256 devices in a mesh: mem: 64 (over x_hi, z, y), lat: 4 (over x_lo, core).
Axes of the slice: x: 4 (x_hi: 2, x_lo: 2; x = x_hi * 2 + x_lo), y: 4, z: 8, core: 2. Of those that a mesh axis runs over, the one named last changes fastest.
Arguments:
- gradient: bfloat16 [720, 5760], P('lat', 'mem'), may hold values from -6 to 6
- perturbations: bfloat16 [64, 720, 5760], P('mem', 'lat'), may hold values from -6 to 6
- lat_mix: float32 [720, 720], replicated, may hold values from -0.21875 to 0.21875
- zonal_weight: float32 [720], replicated, may hold values from 0.05 to 1
Outputs:
- increment: float32 [720, 5760], P('lat', 'mem')
The draws below stay inside these ranges and needn't reach their ends.
All inputs are finite; a program needn't handle non-finite values.
Results may differ from the reference program's by a relative error of at most 0.0003.
Values may be sent and summed in bfloat16 or wider, within the bound.
A program may use at most 128 MiB of HBM per device.

```python
import math
import jax
import jax.numpy as jnp
from jax import lax

NLAT = 720
NLON = 1440
VARS = 4
NWAVE = 720
MEMBERS = 64


def shard_levels(rng, dims, split, least, largest):
    loudness = 1.0
    for dim, shards_of in split:
        steps = jax.random.uniform(jax.random.fold_in(jax.random.fold_in(rng, 6), dim), (shards_of,), jnp.float32, least / len(split), largest / len(split))
        loudness = loudness * jnp.repeat(jnp.exp(steps), dims[dim] // shards_of).reshape((-1,) + (1,) * (len(dims) - 1 - dim))
    return loudness


def bell_draw(own_key, extent, scale, most, pieces=(), kind=jnp.bfloat16):
    values = jax.random.normal(own_key, extent, jnp.float32) * scale
    if len(pieces) > 0:
        values = shard_levels(own_key, extent, pieces, -0.22, 0.18) * values
    return jnp.clip(values, min=-most, max=most).astype(kind)


def setup_inputs(seed: int = 0) -> dict:
    key_list = jax.random.split(jax.random.key(seed), 5)
    gradient = bell_draw(key_list[0], (NLAT, VARS * NLON), 1.0, 6.0, ((0, 4), (1, 64)))
    perturbations = bell_draw(key_list[1], (MEMBERS, NLAT, VARS * NLON), 1.0, 6.0, ((0, 64), (1, 4)))
    lat_mix = bell_draw(key_list[2], (NLAT, NLAT), NLAT ** -0.5, 0.21875, (), jnp.float32)
    zonal_weight = jnp.clip(jnp.exp(jax.random.uniform(key_list[3], (NWAVE,), jnp.float32, math.log(0.05), math.log(1.0))), 0.05, 1.0)
    return {"gradient": gradient, "perturbations": perturbations, "lat_mix": lat_mix, "zonal_weight": zonal_weight}


def dft_tables():
    points = jnp.arange(NLON, dtype=jnp.int32)
    waves = jnp.arange(NWAVE, dtype=jnp.int32)
    angles = (points[:, None] * waves[None, :] % NLON).astype(jnp.float32) * (2.0 * math.pi / NLON)
    cosine = jnp.cos(angles)
    sine = jnp.sin(angles)
    forward = jnp.concatenate([cosine, sine], axis=1)
    weights = jnp.where(waves == 0, 1.0, 2.0).astype(jnp.float32) / NLON
    inverse = jnp.concatenate([cosine.T * weights[:, None], sine.T * weights[:, None]], axis=0)
    return (forward, inverse)

def reference(gradient, perturbations, lat_mix, zonal_weight):
    forward, inverse = dft_tables()
    column_weight = jnp.concatenate([zonal_weight, zonal_weight])
    grad_float = gradient.astype(jnp.float32)
    highest = lax.Precision.HIGHEST

    def member(running, member_row):
        values = member_row.astype(jnp.float32)
        alphas = lax.optimization_barrier(jnp.sum((values * grad_float).reshape(NLAT, VARS, NLON), axis=1))
        spectra = jnp.dot(alphas, forward, precision=highest)
        localized = (spectra + jnp.dot(lat_mix, spectra, precision=highest)) * column_weight
        restored = jnp.dot(localized, inverse, precision=highest)
        term = (values.reshape(NLAT, VARS, NLON) * restored[:, None, :]).reshape(NLAT, VARS * NLON)
        return (running + term, None)
    running, unused = lax.scan(member, jnp.zeros((NLAT, VARS * NLON), jnp.float32), perturbations)
    return running * (1.0 / math.sqrt(MEMBERS - 1))
```

```python
import math

import jax
import jax.numpy as jnp
import numpy as np
from jax import lax
from jax.experimental import pallas as pl
from jax.experimental.pallas import tpu as pltpu
from jax.sharding import PartitionSpec as P

MESH = pl.DeviceIdType.MESH
F32 = jnp.float32
BF16 = jnp.bfloat16
NLON = 1440
NWAVE = 720
MEMBERS = 64
ROWS = 180
HALF = 96
BAND = 192
UNIT = 90
WIDE = 360
LANES = 384
NZ, NY = 8, 4
LEFT = 384
TABLE = 1920


def wave_table():
    waves = np.arange(NWAVE)
    offsets = np.arange(TABLE) - LEFT
    gains = np.where(waves == 0, 1.0, 2.0) / NLON
    angles = (waves[:, None] * offsets[None, :] % NLON) * (2.0 * math.pi / NLON)
    return (gains[:, None] * np.cos(angles)).astype(np.float32)


class Copies:
    def __init__(self, send, recv):
        self.send, self.recv, self.count, self.made = send, recv, 0, []

    def start(self, src, dst, device):
        k = self.count
        self.count += 1
        copy = pltpu.make_async_remote_copy(
            src_ref=src,
            dst_ref=dst,
            send_sem=self.send.at[k],
            recv_sem=self.recv.at[k],
            device_id=device,
            device_id_type=MESH,
        )
        copy.start()
        self.made.append(copy)
        return copy


def gather_ring(copies, n, me, buf, half, plus, minus):
    k = n // 2
    up = copies.start(buf.at[me], buf.at[me], plus)
    down = copies.start(buf.at[me], buf.at[me], minus)
    for t in range(1, k):
        yield
        up_src = lax.rem(me - t + n, n)
        down_src = lax.rem(me + t, n)
        last = t == k - 1
        up.wait_recv()
        part = buf.at[up_src, pl.ds(0, half)] if last else buf.at[up_src]
        up = copies.start(part, part, plus)
        down.wait_recv()
        part = buf.at[down_src, pl.ds(half, half)] if last else buf.at[down_src]
        down = copies.start(part, part, minus)
    yield
    up.wait_recv()
    down.wait_recv()


def scatter_ring(copies, n, me, own, slots, half, plus, minus, finish):
    k = n // 2
    size = 2 * half
    up_slots, down_slots = slots.at[0], slots.at[1]
    far = lax.rem(me + k, n)
    for j in range(half):
        up_slots[k, j] = own(far, j)
        down_slots[k, half + j] = own(far, half + j)
    up = copies.start(
        up_slots.at[k, pl.ds(0, half)], up_slots.at[0, pl.ds(0, half)], plus
    )
    down = copies.start(
        down_slots.at[k, pl.ds(half, half)], down_slots.at[0, pl.ds(half, half)], minus
    )
    for t in range(1, k):
        yield
        up_dest = lax.rem(me + k - t, n)
        down_dest = lax.rem(me - k + t + n, n)
        up.wait_recv()
        for j in range(size):
            if t == 1 and j >= half:
                up_slots[t - 1, j] = own(up_dest, j)
            else:
                up_slots[t - 1, j] += own(up_dest, j)
        up = copies.start(up_slots.at[t - 1], up_slots.at[t], plus)
        down.wait_recv()
        for j in range(size):
            if t == 1 and j < half:
                down_slots[t - 1, j] = own(down_dest, j)
            else:
                down_slots[t - 1, j] += own(down_dest, j)
        down = copies.start(down_slots.at[t - 1], down_slots.at[t], minus)
    yield
    up.wait_recv()
    down.wait_recv()
    for j in range(size):
        finish(j, up_slots[k - 1, j] + down_slots[k - 1, j] + own(me, j))


def kernel(
    pert, grad, mix, weight, table, out,
    p_v, m_v, e_v, unit, yu, zu, gz, gy, pz, py, work, a32, ay, ag,
    mpad, mh, ml, ch, cl, rest, rest_y, s1, s2, s3, s4, t1, t2, ux, ur,
    local_sem, send_sem, recv_sem,
):
    mem, lat = lax.axis_index("mem"), lax.axis_index("lat")
    xh, z, y = mem // 32, (mem // 4) % NZ, mem % NY

    def member(xh_, z_, y_):
        return {"mem": xh_ * 32 + z_ * 4 + y_, "lat": lat}

    z_up, z_down = member(xh, (z + 1) % NZ, y), member(xh, (z + NZ - 1) % NZ, y)
    y_up, y_down = member(xh, z, (y + 1) % NY), member(xh, z, (y + NY - 1) % NY)
    x_far = member(1 - xh, z, y)
    chip_lat = (lat + 2) % 4
    core_lat = lat + 1 - 2 * (lat % 2)
    chip = {"mem": mem, "lat": chip_lat}
    core = {"mem": mem, "lat": core_lat}
    copies = Copies(send_sem, recv_sem)

    loads = [
        pltpu.make_async_copy(table, e_v, local_sem.at[0]),
        pltpu.make_async_copy(pert, p_v, local_sem.at[1]),
        pltpu.make_async_copy(mix, m_v, local_sem.at[2]),
    ]
    for load in loads:
        load.start()

    barrier = pltpu.get_barrier_semaphore()
    peers = (z_up, z_down, y_up, y_down, x_far, chip, core)
    for peer in peers:
        pl.semaphore_signal(barrier, inc=1, device_id=peer, device_id_type=MESH)
    unit[xh] = jnp.zeros((BAND, 128), BF16)
    unit[xh, 0:ROWS, 0:UNIT] = grad[...]
    pl.semaphore_wait(barrier, len(peers))

    x_copy = copies.start(unit.at[xh], unit.at[xh], x_far)

    tail = jnp.zeros((HALF, LANES - WIDE), BF16)
    for q in range(2 * NZ):
        pz[q, :, WIDE:] = tail
    for i in range(NY):
        a32[i, :, WIDE:] = jnp.zeros((BAND, LANES - WIDE), F32)
        rest_y[i, :, WIDE:] = jnp.zeros((HALF, LANES - WIDE), F32)
        for v in range(4):
            py[i, v, :, WIDE:] = tail
            py[i, v, 84:, :] = jnp.zeros((HALF - 84, LANES), BF16)
    for i in range(2):
        gz[z, i, :, WIDE:] = tail
    for v in range(4):
        gy[y, v, :, WIDE:] = tail

    def color_one():
        for i in range(2):
            yu[y, i] = unit[i, 0:HALF]
        yield from gather_ring(copies, NY, y, yu, 1, y_up, y_down)
        for i in range(2):
            for j in range(NY):
                gz[z, i, :, UNIT * j : UNIT * (j + 1)] = yu[j, i, :, 0:UNIT]
        yield from gather_ring(copies, NZ, z, gz, 1, z_up, z_down)

    def color_two():
        for i in range(2):
            zu[z, i] = unit[i, HALF:BAND]
        yield from gather_ring(copies, NZ, z, zu, 1, z_up, z_down)
        for i in range(2):
            for j in range(NZ):
                v, r = 2 * i + j // 4, j % 4
                gy[y, v, :, UNIT * r : UNIT * (r + 1)] = zu[j, i, :, 0:UNIT]
        yield from gather_ring(copies, NY, y, gy, 2, y_up, y_down)

    def stage_pz(v):
        if v == 0:
            loads[1].wait()
        for r in range(4):
            q = 4 * v + r
            pz[q, :, 0:WIDE] = p_v[0:HALF, WIDE * q : WIDE * (q + 1)]

    def stage_py(v):
        for i in range(NY):
            for r in range(4):
                c = WIDE * (4 * v + r) + UNIT * i
                py[i, v, 0:84, UNIT * r : UNIT * (r + 1)] = p_v[HALF:ROWS, c : c + UNIT]

    def stage_mix():
        loads[2].wait()
        odd = lat % 2
        first = pl.multiple_of(ROWS * lat - 4 * odd, 8)
        rows = m_v[pl.ds(first, ROWS + 4), :]
        rows = jnp.where(odd == 1, rows[4:], rows[:ROWS])
        mpad[...] = jnp.zeros((BAND, 4 * BAND), F32)
        for b in range(4):
            mpad[0:ROWS, BAND * b : BAND * b + ROWS] = rows[:, ROWS * b : ROWS * (b + 1)]
        full = mpad[...]
        high = full.astype(BF16)
        mh[...] = high
        ml[...] = (full - high.astype(F32)).astype(BF16)

    def stage_lags():
        loads[0].wait()
        row = jnp.broadcast_to(weight[...].reshape(1, NWAVE), (8, NWAVE))
        work[...] = jnp.dot(
            row, e_v[...], precision=lax.Precision.HIGHEST, preferred_element_type=F32
        )

    def stage_kernel(d):
        lags = jnp.concatenate(
            [
                work[0:1, LEFT + WIDE * d : LEFT + WIDE * d + LANES],
                work[0:1, WIDE * d : WIDE * d + LEFT],
            ],
            axis=1,
        )
        turned = pltpu.roll(
            jnp.broadcast_to(lags, (LANES, 2 * LANES)), 0, 1, stride=1, stride_axis=0
        )
        block = turned[:, :LANES]
        high = block.astype(BF16)
        low = (block - high.astype(F32)).astype(BF16)
        for r in range(4):
            s = (r + d) % 4
            ch[r, :, LANES * s : LANES * (s + 1)] = high
            cl[r, :, LANES * s : LANES * (s + 1)] = low

    stage_lags()
    x_copy.wait_recv()
    one, two = color_one(), color_two()
    next(one)
    next(two)
    stage_pz(0)
    next(one)
    next(two)
    stage_pz(1)
    next(one)
    next(two)
    stage_pz(2)
    next(two)
    stage_pz(3)
    next(one)
    next(two)
    stage_py(0)
    stage_py(1)
    stage_mix()
    next(one)
    stage_py(2)
    stage_py(3)
    stage_kernel(0)
    next(one)
    stage_kernel(1)
    next(two)
    stage_kernel(2)
    stage_kernel(3)
    next(one, None)
    for r in range(4):
        total = jnp.zeros((HALF, LANES), F32)
        for v in range(4):
            total += pz[4 * v + r].astype(F32) * gz[r + 4 * (v % 2), v // 2].astype(F32)
        a32[r, 0:HALF] = total
    next(two, None)
    for i in range(NY):
        total = jnp.zeros((HALF, LANES), F32)
        for v in range(4):
            total += py[i, v].astype(F32) * gy[i, v].astype(F32)
        ay[i] = total

    def band_rows(b):
        return pl.ds(pl.multiple_of(BAND * b, BAND), BAND)

    to_chip, to_core, passed = [], [], []
    for r in range(4):
        for i in range(NY):
            a32[r, HALF:BAND, UNIT * i : UNIT * (i + 1)] = ay[
                i, :, UNIT * r : UNIT * (r + 1)
            ]
        value = a32[r]
        high = value.astype(BF16)
        ag[r, band_rows(lat), 0:LANES] = high
        ag[r, band_rows(lat), LANES:] = (value - high.astype(F32)).astype(BF16)
        here = ag.at[r, band_rows(lat)]
        to_chip.append(copies.start(here, here, chip))
        to_core.append(copies.start(here, here, core))

    def localize(r):
        to_core[r].wait_recv()
        passed[r].wait_recv()
        both = jnp.dot(mh[...], ag[r], preferred_element_type=F32)
        low = jnp.dot(ml[...], ag[r, :, 0:LANES], preferred_element_type=F32)
        mixed = a32[r] + (both[:, :LANES] + (both[:, LANES:] + low))
        high = mixed.astype(BF16)
        low = (mixed - high.astype(F32)).astype(BF16)
        for s in range(4):
            cols = slice(LANES * s, LANES * (s + 1))
            term = jnp.dot(high, ch[r, :, cols], preferred_element_type=F32) + (
                jnp.dot(high, cl[r, :, cols], preferred_element_type=F32)
                + jnp.dot(low, ch[r, :, cols], preferred_element_type=F32)
            )
            if r == 0:
                rest[s] = term
            else:
                rest[s] += term

    for r in range(4):
        to_chip[r].wait_recv()
        there = ag.at[r, band_rows(chip_lat)]
        passed.append(copies.start(there, there, core))
        if r > 0:
            localize(r - 1)
    localize(3)

    def own_one(d, j):
        return pz[j * NZ + d].astype(F32) * rest[d % 4, 0:HALF]

    def own_two(d, j):
        return py[d, j].astype(F32) * rest_y[d]

    def store_one(j, value):
        for i in range(NY):
            t1[i, j, :, 0:UNIT] = value[:, UNIT * i : UNIT * (i + 1)]

    def store_two(j, value):
        for r in range(4):
            t2[r + 4 * (j % 2), j // 2, :, 0:UNIT] = value[:, UNIT * r : UNIT * (r + 1)]

    def last_one(j, value):
        ux[j, 0:HALF] = value

    def last_two(j, value):
        ux[j, HALF:BAND] = value

    def sum_one():
        yield from scatter_ring(copies, NZ, z, own_one, s1, 1, z_up, z_down, store_one)
        yield from scatter_ring(
            copies, NY, y, lambda d, j: t1[d, j], s3, 1, y_up, y_down, last_one
        )

    def sum_two():
        for i in range(NY):
            for r in range(4):
                rest_y[i, :, UNIT * r : UNIT * (r + 1)] = rest[
                    r, HALF:BAND, UNIT * i : UNIT * (i + 1)
                ]
        yield from scatter_ring(copies, NY, y, own_two, s2, 2, y_up, y_down, store_two)
        yield from scatter_ring(
            copies, NZ, z, lambda d, j: t2[d, j], s4, 1, z_up, z_down, last_two
        )

    one, two = sum_one(), sum_two()
    for chain in (one, two, one, two, one, one, two, two, one, two, two, one, one, two):
        next(chain, None)
    x_copy = copies.start(ux.at[1 - xh], ur, x_far)
    x_copy.wait_recv()
    total = (ux[xh] + ur[...]) * (1.0 / math.sqrt(MEMBERS - 1))
    out[...] = total[0:ROWS, 0:UNIT]
    for copy in copies.made:
        copy.wait_send()


def local(gradient, perturbations, lat_mix, zonal_weight):
    vmem = pl.BlockSpec(memory_space=pltpu.VMEM)
    hbm = pl.BlockSpec(memory_space=pl.ANY)
    return pl.pallas_call(
        kernel,
        out_shape=jax.ShapeDtypeStruct((ROWS, UNIT), F32),
        in_specs=[hbm, vmem, hbm, vmem, hbm],
        out_specs=vmem,
        scratch_shapes=[
            pltpu.VMEM((ROWS, 4 * NLON), BF16),
            pltpu.VMEM((720, 720), F32),
            pltpu.VMEM((NWAVE, TABLE), F32),
            pltpu.VMEM((2, BAND, 128), BF16),
            pltpu.VMEM((NY, 2, HALF, 128), BF16),
            pltpu.VMEM((NZ, 2, HALF, 128), BF16),
            pltpu.VMEM((NZ, 2, HALF, LANES), BF16),
            pltpu.VMEM((NY, 4, HALF, LANES), BF16),
            pltpu.VMEM((2 * NZ, HALF, LANES), BF16),
            pltpu.VMEM((NY, 4, HALF, LANES), BF16),
            pltpu.VMEM((8, TABLE), F32),
            pltpu.VMEM((4, BAND, LANES), F32),
            pltpu.VMEM((NY, HALF, LANES), F32),
            pltpu.VMEM((4, 4 * BAND, 2 * LANES), BF16),
            pltpu.VMEM((BAND, 4 * BAND), F32),
            pltpu.VMEM((BAND, 4 * BAND), BF16),
            pltpu.VMEM((BAND, 4 * BAND), BF16),
            pltpu.VMEM((4, LANES, 4 * LANES), BF16),
            pltpu.VMEM((4, LANES, 4 * LANES), BF16),
            pltpu.VMEM((4, BAND, LANES), F32),
            pltpu.VMEM((NY, HALF, LANES), F32),
            pltpu.VMEM((2, NZ // 2 + 1, 2, HALF, LANES), F32),
            pltpu.VMEM((2, NY // 2 + 1, 4, HALF, LANES), F32),
            pltpu.VMEM((2, NY // 2 + 1, 2, HALF, 128), F32),
            pltpu.VMEM((2, NZ // 2 + 1, 2, HALF, 128), F32),
            pltpu.VMEM((NY, 2, HALF, 128), F32),
            pltpu.VMEM((NZ, 2, HALF, 128), F32),
            pltpu.VMEM((2, BAND, 128), F32),
            pltpu.VMEM((BAND, 128), F32),
            pltpu.SemaphoreType.DMA((3,)),
            pltpu.SemaphoreType.DMA((64,)),
            pltpu.SemaphoreType.DMA((64,)),
        ],
        compiler_params=pltpu.CompilerParams(
            collective_id=0, has_side_effects=True, vmem_limit_bytes=56 * 2**20
        ),
    )(
        perturbations.reshape(ROWS, 4 * NLON),
        gradient,
        lat_mix,
        zonal_weight,
        jnp.asarray(wave_table()),
    )


def solution(mesh):
    return jax.shard_map(
        local,
        mesh=mesh,
        in_specs=(P("lat", "mem"), P("mem", "lat", None), P(), P()),
        out_specs=P("lat", "mem"),
        check_vma=False,
    )
```

```python
import math

import jax
import jax.numpy as jnp
import numpy as np
from jax import lax
from jax.experimental import pallas as pl
from jax.experimental.pallas import tpu as pltpu
from jax.sharding import PartitionSpec as P

MESH = pl.DeviceIdType.MESH
F32 = jnp.float32
BF16 = jnp.bfloat16
NLON = 1440
NWAVE = 720
MEMBERS = 64
ROWS = 180
BAND = 192
ONE = 112
TWO = BAND - ONE
REAL = ROWS - ONE
FLOAT = (REAL + 7) // 8 * 8
UNIT = 90
WIDE = 360
LANES = 384
NZ, NY = 8, 4
LEFT = 384
TABLE = 1920


def wave_table():
    waves = np.arange(NWAVE)
    offsets = np.arange(TABLE) - LEFT
    gains = np.where(waves == 0, 1.0, 2.0) / NLON
    angles = (waves[:, None] * offsets[None, :] % NLON) * (2.0 * math.pi / NLON)
    return (gains[:, None] * np.cos(angles)).astype(np.float32)


class Copies:
    def __init__(self, send, recv):
        self.send, self.recv, self.count, self.made = send, recv, 0, []

    def start(self, src, dst, device):
        k = self.count
        self.count += 1
        copy = pltpu.make_async_remote_copy(
            src_ref=src,
            dst_ref=dst,
            send_sem=self.send.at[k],
            recv_sem=self.recv.at[k],
            device_id=device,
            device_id_type=MESH,
        )
        copy.start()
        self.made.append(copy)
        return copy


def gather_ring(copies, n, me, buf, half, plus, minus):
    k = n // 2
    parts = (pl.ds(0, half), pl.ds(half, half))
    up, down = {}, {}
    for j in (0, 1):
        mine = buf.at[me, parts[j]]
        up[j] = copies.start(mine, mine, plus)
        down[1 - j] = copies.start(
            buf.at[me, parts[1 - j]], buf.at[me, parts[1 - j]], minus
        )
    for t in range(1, k):
        yield t
        for j in (0, 1):
            i = 1 - j
            up[j].wait_recv()
            if t < k - 1 or j == 0:
                there = buf.at[lax.rem(me - t + n, n), parts[j]]
                up[j] = copies.start(there, there, plus)
            down[i].wait_recv()
            if t < k - 1 or i == 1:
                there = buf.at[lax.rem(me + t, n), parts[i]]
                down[i] = copies.start(there, there, minus)
    yield k
    up[0].wait_recv()
    down[1].wait_recv()


def scatter_ring(copies, n, me, own, first, slots, half, plus, minus, finish):
    k = n // 2
    low, high = range(half), range(half, 2 * half)
    up, down = {}, {}

    def begin(way, dest, j, t, device, made):
        first[way, j] = own(dest, j)
        made[j] = copies.start(first.at[way, j], slots.at[way, t, j], device)

    def forward(way, dest, j, t, device, made):
        made[j].wait_recv()
        slots[way, t - 1, j] += own(dest, j)
        made[j] = copies.start(slots.at[way, t - 1, j], slots.at[way, t, j], device)

    for a, b in zip(low, high):
        begin(0, lax.rem(me + k, n), a, 0, plus, up)
        begin(1, lax.rem(me + k, n), b, 0, minus, down)
    for a, b in zip(low, high):
        begin(0, lax.rem(me + k - 1, n), b, 1, plus, up)
        begin(1, lax.rem(me - k + 1 + n, n), a, 1, minus, down)
    for t in range(1, k):
        yield
        up_dest = lax.rem(me + k - t, n)
        down_dest = lax.rem(me - k + t + n, n)
        if t > 1:
            for a, b in zip(low, high):
                forward(0, up_dest, b, t, plus, up)
                forward(1, down_dest, a, t, minus, down)
        for a, b in zip(low, high):
            forward(0, up_dest, a, t, plus, up)
            forward(1, down_dest, b, t, minus, down)
    yield
    for j in (*high, *low):
        up[j].wait_recv()
        down[j].wait_recv()
        finish(j, slots[0, k - 1, j] + slots[1, k - 1, j] + own(me, j))


def kernel(
    pert, grad, mix, weight, table, out,
    p_v, m_v, e_v, yu, zu, gz, gy, pz, py, work, own_two, ag_one, ag_two,
    mpad, mh_one, ml_one, mh_two, ml_two, ch, cl, local, rest, rest_y,
    f1, s1, f2, s2, s4, t1, t2, p1, p2,
    local_sem, send_sem, recv_sem,
):
    mem, lat = lax.axis_index("mem"), lax.axis_index("lat")
    xh, z, y = mem // 32, (mem // 4) % NZ, mem % NY

    def member(dx, dz, dy):
        there = (
            lax.rem(xh + dx, 2) * 32 + lax.rem(z + dz, NZ) * 4 + lax.rem(y + dy, NY)
        )
        return {"mem": there, "lat": lat}

    z_up, z_down = member(0, 1, 0), member(0, NZ - 1, 0)
    y_up, y_down = member(0, 0, 1), member(0, 0, NY - 1)
    x_far, x_up, x_down = member(1, 0, 0), member(1, 1, 0), member(1, NZ - 1, 0)
    chip_lat = lax.rem(lat + 2, 4)
    chip = {"mem": mem, "lat": chip_lat}
    core = {"mem": mem, "lat": lat + 1 - 2 * lax.rem(lat, 2)}
    plane = [(dx, dy) for dx in range(2) for dy in range(NY) if (dx, dy) != (0, 0)]
    copies = Copies(send_sem, recv_sem)

    loads = [
        pltpu.make_async_copy(pert, p_v, local_sem.at[0]),
        pltpu.make_async_copy(table, e_v, local_sem.at[1]),
        pltpu.make_async_copy(mix, m_v, local_sem.at[2]),
    ]
    for load in loads:
        load.start()

    barrier = pltpu.get_barrier_semaphore()
    peers = [member(dx, 0, dy) for dx, dy in plane]
    peers += [z_up, z_down, x_up, x_down, chip, core]
    for peer in peers:
        pl.semaphore_signal(barrier, inc=1, device_id=peer, device_id_type=MESH)
    yu[xh, y] = jnp.zeros((ONE, 128), BF16)
    yu[xh, y, :, 0:UNIT] = grad[0:ONE]
    zu[z, xh] = jnp.zeros((TWO, 128), BF16)
    zu[z, xh, 0:REAL, 0:UNIT] = grad[ONE:ROWS]
    pl.semaphore_wait(barrier, len(peers))

    pieces = []

    def band_rows(b, rows):
        return pl.ds(pl.multiple_of(b * rows, 16), rows)

    def send_piece(ag, index, rows, value):
        high = value.astype(BF16)
        ag[index, band_rows(lat, rows), 0:LANES] = high
        ag[index, band_rows(lat, rows), LANES:] = (value - high.astype(F32)).astype(BF16)
        here = ag.at[index, band_rows(lat, rows)]
        there = ag.at[index, band_rows(chip_lat, rows)]
        pieces.append(
            {
                "index": index,
                "one": rows == ONE,
                "there": there,
                "chip": copies.start(here, here, chip),
                "core": copies.start(here, here, core),
            }
        )

    def pass_piece(k):
        piece = pieces[k]
        piece["chip"].wait_recv()
        piece["passed"] = copies.start(piece["there"], piece["there"], core)

    def mixed(high, low, ag, index):
        both = jnp.dot(high[...], ag[index], preferred_element_type=F32)
        return both[:, :LANES] + (
            both[:, LANES:]
            + jnp.dot(low[...], ag[index, :, 0:LANES], preferred_element_type=F32)
        )

    def mix_piece(k):
        piece = pieces[k]
        piece["core"].wait_recv()
        piece["passed"].wait_recv()
        index = piece["index"]
        if piece["one"]:
            local[index] += mixed(mh_one, ml_one, ag_one, index)
        else:
            work_y[...] = mixed(mh_two, ml_two, ag_two, index)
            for i in range(NY):

                @pl.when(index == i)
                def _():
                    for r in range(4):
                        local[r, :, UNIT * i : UNIT * (i + 1)] += work_y[
                            :, UNIT * r : UNIT * (r + 1)
                        ]

    work_y = own_two

    def piece_one(r):
        total = jnp.zeros((ONE, LANES), F32)
        for v in range(4):
            total += pz[4 * v + r].astype(F32) * gz[r + 4 * (v % 2), v // 2].astype(F32)
        send_piece(ag_one, r, ONE, total)
        local[r, 0:ONE] += total

    def piece_two(i):
        total = jnp.zeros((TWO, LANES), F32)
        for v in range(4):
            total += py[i, v].astype(F32) * gy[i, v].astype(F32)
        send_piece(ag_two, i, TWO, total)
        own_two[0:TWO] = total
        for i_ in range(NY):

            @pl.when(i == i_)
            def _():
                for r in range(4):
                    local[r, ONE:BAND, UNIT * i_ : UNIT * (i_ + 1)] += own_two[
                        0:TWO, UNIT * r : UNIT * (r + 1)
                    ]

    def color_one():
        mine = yu.at[xh, y]
        arriving = [copies.start(mine, mine, member(dx, 0, dy)) for dx, dy in plane]
        yield
        for copy in arriving:
            copy.wait_recv()
        for i in range(2):
            for j in range(NY):
                gz[z, i, :, UNIT * j : UNIT * (j + 1)] = yu[i, j, :, 0:UNIT]
        for t in gather_ring(copies, NZ, z, gz, 1, z_up, z_down):
            if t == 3:
                piece_one(lax.rem(z + 2, 4))
            if t == 4:
                piece_one(lax.rem(z + 1, 4))
                piece_one(lax.rem(z + 3, 4))
            yield
        piece_one(lax.rem(z, 4))

    def color_two():
        mine = zu.at[z, xh]
        up = [copies.start(mine, mine, z_up)]
        down = [copies.start(mine, mine, z_down)]
        far = copies.start(mine, mine, x_far)
        up.append(copies.start(mine, mine, x_up))
        down.append(copies.start(mine, mine, x_down))
        for t in range(1, NZ // 2):
            yield
            for copy in up:
                copy.wait_recv()
            there = zu.at[lax.rem(z + NZ - t, NZ)]
            if t == NZ // 2 - 1:
                there = zu.at[lax.rem(z + NZ - t, NZ), pl.ds(0, 1)]
            up = [copies.start(there, there, z_up)]
            for copy in down:
                copy.wait_recv()
            there = zu.at[lax.rem(z + t, NZ)]
            if t == NZ // 2 - 1:
                there = zu.at[lax.rem(z + t, NZ), pl.ds(1, 1)]
            down = [copies.start(there, there, z_down)]
        yield
        for copy in (far, *up, *down):
            copy.wait_recv()
        for i in range(2):
            for j in range(NZ):
                v, r = 2 * i + j // 4, j % 4
                gy[y, v, :, UNIT * r : UNIT * (r + 1)] = zu[j, i, :, 0:UNIT]
        for t in gather_ring(copies, NY, y, gy, 2, y_up, y_down):
            if t == 1:
                piece_two(y)
            if t == 2:
                piece_two(lax.rem(y + 1, NY))
                piece_two(lax.rem(y + 3, NY))
            yield
        piece_two(lax.rem(y + 2, NY))

    def stage_zeros():
        for q in range(2 * NZ):
            pz[q, :, WIDE:] = jnp.zeros((ONE, LANES - WIDE), BF16)
        for i in range(NY):
            local[i] = jnp.zeros((BAND, LANES), F32)
            rest_y[i, :, WIDE:] = jnp.zeros((FLOAT, LANES - WIDE), F32)
            for v in range(4):
                py[i, v, :, WIDE:] = jnp.zeros((TWO, LANES - WIDE), BF16)
                py[i, v, REAL:, :] = jnp.zeros((TWO - REAL, LANES), BF16)
        for i in range(2):
            gz[z, i, :, WIDE:] = jnp.zeros((ONE, LANES - WIDE), BF16)
        for v in range(4):
            gy[y, v, :, WIDE:] = jnp.zeros((TWO, LANES - WIDE), BF16)

    def stage_pz(v):
        for r in range(4):
            q = 4 * v + r
            pz[q, :, 0:WIDE] = p_v[0:ONE, WIDE * q : WIDE * (q + 1)]

    def stage_py(v):
        for i in range(NY):
            for r in range(4):
                c = WIDE * (4 * v + r) + UNIT * i
                py[i, v, 0:REAL, UNIT * r : UNIT * (r + 1)] = p_v[ONE:ROWS, c : c + UNIT]

    def stage_mix():
        loads[2].wait()
        odd = lax.rem(lat, 2)
        first = pl.multiple_of(ROWS * lat - 4 * odd, 8)
        rows = m_v[pl.ds(first, ROWS + 4), :]
        rows = jnp.where(odd == 1, rows[4:], rows[:ROWS])
        mpad[...] = jnp.zeros((BAND, 4 * BAND), F32)
        for b in range(4):
            c = ROWS * b
            mpad[0:ROWS, ONE * b : ONE * (b + 1)] = rows[:, c : c + ONE]
            d = 4 * ONE + TWO * b
            mpad[0:ROWS, d : d + REAL] = rows[:, c + ONE : c + ROWS]
        for high, low, full in (
            (mh_one, ml_one, mpad[:, 0 : 4 * ONE]),
            (mh_two, ml_two, mpad[:, 4 * ONE :]),
        ):
            rounded = full.astype(BF16)
            high[...] = rounded
            low[...] = (full - rounded.astype(F32)).astype(BF16)

    def stage_lags():
        loads[1].wait()
        row = jnp.broadcast_to(weight[...].reshape(1, NWAVE), (8, NWAVE))
        work[...] = jnp.dot(
            row, e_v[...], precision=lax.Precision.HIGHEST, preferred_element_type=F32
        )

    def stage_kernel(d):
        lags = jnp.concatenate(
            [
                work[0:1, LEFT + WIDE * d : LEFT + WIDE * d + LANES],
                work[0:1, WIDE * d : WIDE * d + LEFT],
            ],
            axis=1,
        )
        turned = pltpu.roll(
            jnp.broadcast_to(lags, (LANES, 2 * LANES)), 0, 1, stride=1, stride_axis=0
        )
        block = turned[:, :LANES]
        high = block.astype(BF16)
        low = (block - high.astype(F32)).astype(BF16)
        for r in range(4):
            s = (r + d) % 4
            place = (
                slice(LANES * r, LANES * (r + 1)),
                slice(LANES * s, LANES * (s + 1)),
            )
            ch[place] = high
            cl[place] = low

    one, two = color_one(), color_two()
    next(one)
    next(two)
    stage_zeros()
    loads[0].wait()
    stage_pz(0)
    next(one)
    stage_pz(1)
    next(two)
    stage_pz(2)
    stage_pz(3)
    next(one)
    next(two)
    stage_py(0)
    stage_py(1)
    next(two)
    next(one)
    stage_py(2)
    stage_py(3)
    next(two)
    next(one)
    stage_mix()
    stage_lags()
    pass_piece(0)
    next(one, None)
    stage_kernel(0)
    pass_piece(1)
    stage_kernel(1)
    pass_piece(2)
    next(two)
    stage_kernel(2)
    stage_kernel(3)
    next(two, None)
    pass_piece(3)
    for k in range(4):
        mix_piece(k)
        pass_piece(4 + k)
    for k in range(4, 8):
        mix_piece(k)

    def restore(rows):
        value = jnp.concatenate([local[r, rows] for r in range(4)], axis=1)
        high = value.astype(BF16)
        low = (value - high.astype(F32)).astype(BF16)
        for s in range(4):
            cols = slice(LANES * s, LANES * (s + 1))
            rest[s, rows] = jnp.dot(high, ch[:, cols], preferred_element_type=F32) + (
                jnp.dot(high, cl[:, cols], preferred_element_type=F32)
                + jnp.dot(low, ch[:, cols], preferred_element_type=F32)
            )

    def term_one(d, j):
        return pz[j * NZ + d].astype(F32) * rest[lax.rem(d, 4), 0:ONE]

    def term_two(d, j):
        return py[d, j, 0:FLOAT].astype(F32) * rest_y[d]

    def store_one(j, value):
        for i in range(NY):
            t1[j, i, :, 0:UNIT] = value[:, UNIT * i : UNIT * (i + 1)]

    def store_two(j, value):
        for r in range(4):
            t2[r + 4 * (j % 2), j // 2, :, 0:UNIT] = value[:, UNIT * r : UNIT * (r + 1)]

    scale = 1.0 / math.sqrt(MEMBERS - 1)

    def sum_one():
        restore(slice(0, ONE))
        yield from scatter_ring(
            copies, NZ, z, term_one, f1, s1, 1, z_up, z_down, store_one
        )
        arriving = []
        for k, (dx, dy) in enumerate(plane):
            part = t1.at[lax.rem(xh + dx, 2), lax.rem(y + dy, NY)]
            arriving.append(copies.start(part, p1.at[k], member(dx, 0, dy)))
        yield
        total = t1[xh, y]
        for k, copy in enumerate(arriving):
            copy.wait_recv()
            total += p1[k]
        out[0:ONE, :] = (total * scale)[:, 0:UNIT]

    def sum_two():
        restore(slice(ONE, BAND))
        for i in range(NY):
            for r in range(4):
                rest_y[i, :, UNIT * r : UNIT * (r + 1)] = rest[
                    r, ONE : ONE + FLOAT, UNIT * i : UNIT * (i + 1)
                ]
        yield from scatter_ring(
            copies, NY, y, term_two, f2, s2, 2, y_up, y_down, store_two
        )
        last = NZ // 2 - 1
        far = lax.rem(z + NZ // 2, NZ)
        cross = copies.start(t2.at[z, 1 - xh], p2.at[4], x_far)
        up = copies.start(t2.at[far, pl.ds(0, 1)], s4.at[0, 0, pl.ds(0, 1)], z_up)
        down = copies.start(t2.at[far, pl.ds(1, 1)], s4.at[1, 0, pl.ds(1, 1)], z_down)
        for t in range(1, NZ // 2):
            yield
            made = []
            for way, copy, dest, near, aside in (
                (0, up, lax.rem(z + NZ // 2 - t, NZ), z_up, x_up),
                (1, down, lax.rem(z + NZ // 2 + t, NZ), z_down, x_down),
            ):
                copy.wait_recv()
                for j in range(2):
                    if t == 1 and j != way:
                        s4[way, t - 1, j] = t2[dest, j]
                    else:
                        s4[way, t - 1, j] += t2[dest, j]
                if t < last:
                    made.append(copies.start(s4.at[way, t - 1], s4.at[way, t], near))
                else:
                    made.append(
                        (
                            copies.start(s4.at[way, t - 1, xh], p2.at[2 * way], near),
                            copies.start(
                                s4.at[way, t - 1, 1 - xh], p2.at[2 * way + 1], aside
                            ),
                        )
                    )
            up, down = made
        yield
        for copy in (cross, *up, *down):
            copy.wait_recv()
        total = t2[z, xh]
        for k in range(5):
            total += p2[k]
        out[ONE:ROWS, :] = (total * scale)[0:REAL, 0:UNIT]

    one, two = sum_one(), sum_two()
    for chain in (one, two, one, two, one, two, one, two, two, one, two, two, one):
        next(chain, None)
    for copy in copies.made:
        copy.wait_send()


def local(gradient, perturbations, lat_mix, zonal_weight):
    vmem = pl.BlockSpec(memory_space=pltpu.VMEM)
    hbm = pl.BlockSpec(memory_space=pl.ANY)
    return pl.pallas_call(
        kernel,
        out_shape=jax.ShapeDtypeStruct((ROWS, UNIT), F32),
        in_specs=[hbm, vmem, hbm, vmem, hbm],
        out_specs=vmem,
        scratch_shapes=[
            pltpu.VMEM((ROWS, 4 * NLON), BF16),
            pltpu.VMEM((720, 720), F32),
            pltpu.VMEM((NWAVE, TABLE), F32),
            pltpu.VMEM((2, NY, ONE, 128), BF16),
            pltpu.VMEM((NZ, 2, TWO, 128), BF16),
            pltpu.VMEM((NZ, 2, ONE, LANES), BF16),
            pltpu.VMEM((NY, 4, TWO, LANES), BF16),
            pltpu.VMEM((2 * NZ, ONE, LANES), BF16),
            pltpu.VMEM((NY, 4, TWO, LANES), BF16),
            pltpu.VMEM((8, TABLE), F32),
            pltpu.VMEM((BAND, LANES), F32),
            pltpu.VMEM((4, 4 * ONE, 2 * LANES), BF16),
            pltpu.VMEM((4, 4 * TWO, 2 * LANES), BF16),
            pltpu.VMEM((BAND, 4 * BAND), F32),
            pltpu.VMEM((BAND, 4 * ONE), BF16),
            pltpu.VMEM((BAND, 4 * ONE), BF16),
            pltpu.VMEM((BAND, 4 * TWO), BF16),
            pltpu.VMEM((BAND, 4 * TWO), BF16),
            pltpu.VMEM((4 * LANES, 4 * LANES), BF16),
            pltpu.VMEM((4 * LANES, 4 * LANES), BF16),
            pltpu.VMEM((4, BAND, LANES), F32),
            pltpu.VMEM((4, BAND, LANES), F32),
            pltpu.VMEM((NY, FLOAT, LANES), F32),
            pltpu.VMEM((2, 2, ONE, LANES), F32),
            pltpu.VMEM((2, NZ // 2, 2, ONE, LANES), F32),
            pltpu.VMEM((2, 4, FLOAT, LANES), F32),
            pltpu.VMEM((2, NY // 2, 4, FLOAT, LANES), F32),
            pltpu.VMEM((2, NZ // 2 - 1, 2, FLOAT, 128), F32),
            pltpu.VMEM((2, NY, ONE, 128), F32),
            pltpu.VMEM((NZ, 2, FLOAT, 128), F32),
            pltpu.VMEM((7, ONE, 128), F32),
            pltpu.VMEM((5, FLOAT, 128), F32),
            pltpu.SemaphoreType.DMA((3,)),
            pltpu.SemaphoreType.DMA((128,)),
            pltpu.SemaphoreType.DMA((128,)),
        ],
        compiler_params=pltpu.CompilerParams(
            collective_id=0, has_side_effects=True, vmem_limit_bytes=56 * 2**20
        ),
    )(
        perturbations.reshape(ROWS, 4 * NLON),
        gradient,
        lat_mix,
        zonal_weight,
        jnp.asarray(wave_table()),
    )


def solution(mesh):
    return jax.shard_map(
        local,
        mesh=mesh,
        in_specs=(P("lat", "mem"), P("mem", "lat", None), P(), P()),
        out_specs=P("lat", "mem"),
        check_vma=False,
    )
```

```python
import math

import jax
import jax.numpy as jnp
import numpy as np
from jax import lax
from jax.experimental import pallas as pl
from jax.experimental.pallas import tpu as pltpu
from jax.sharding import PartitionSpec as P

MESH = pl.DeviceIdType.MESH
F32 = jnp.float32
BF16 = jnp.bfloat16
NLON = 1440
NWAVE = 720
MEMBERS = 64
ROWS = 180
BAND = 192
ONE = 112
CUT = 64
TWO = BAND - ONE
REAL = ROWS - ONE
FLOAT = (REAL + 7) // 8 * 8
UNIT = 90
WIDE = 360
LANES = 384
NZ, NY = 8, 4
LEFT = 384
TABLE = 1920


def wave_table():
    waves = np.arange(NWAVE)
    offsets = np.arange(TABLE) - LEFT
    gains = np.where(waves == 0, 1.0, 2.0) / NLON
    angles = (waves[:, None] * offsets[None, :] % NLON) * (2.0 * math.pi / NLON)
    return (gains[:, None] * np.cos(angles)).astype(np.float32)


class Copies:
    def __init__(self, send, recv):
        self.send, self.recv, self.count, self.made = send, recv, 0, []

    def start(self, src, dst, device):
        k = self.count
        self.count += 1
        copy = pltpu.make_async_remote_copy(
            src_ref=src,
            dst_ref=dst,
            send_sem=self.send.at[k],
            recv_sem=self.recv.at[k],
            device_id=device,
            device_id_type=MESH,
        )
        copy.start()
        self.made.append(copy)
        return copy


def gather_ring(copies, n, me, pick, parts, plus, minus):
    k = n // 2
    early, late = range(parts // 2), range(parts // 2, parts)
    up, down = {}, {}
    for i, j in zip((*early, *late), (*late, *early)):
        up[i] = copies.start(pick(me, i), pick(me, i), plus)
        down[j] = copies.start(pick(me, j), pick(me, j), minus)
    for t in range(1, k):
        yield t
        up_src, down_src = lax.rem(me - t + n, n), lax.rem(me + t, n)
        for i, j in zip((*early, *late), (*late, *early)):
            up[i].wait_recv()
            if t < k - 1 or i in early:
                up[i] = copies.start(pick(up_src, i), pick(up_src, i), plus)
            down[j].wait_recv()
            if t < k - 1 or j in late:
                down[j] = copies.start(pick(down_src, j), pick(down_src, j), minus)
    yield k
    for i, j in zip(early, late):
        up[i].wait_recv()
        down[j].wait_recv()


def scatter_ring(copies, n, me, own, first, slots, half, plus, minus, finish):
    k = n // 2
    low, high = range(half), range(half, 2 * half)
    up, down = {}, {}

    def begin(way, dest, j, t, device, made):
        first[way, j] = own(dest, j)
        made[j] = copies.start(first.at[way, j], slots.at[way, t, j], device)

    def forward(way, dest, j, t, device, made):
        made[j].wait_recv()
        slots[way, t - 1, j] += own(dest, j)
        made[j] = copies.start(slots.at[way, t - 1, j], slots.at[way, t, j], device)

    for a, b in zip(low, high):
        begin(0, lax.rem(me + k, n), a, 0, plus, up)
        begin(1, lax.rem(me + k, n), b, 0, minus, down)
    for a, b in zip(low, high):
        begin(0, lax.rem(me + k - 1, n), b, 1, plus, up)
        begin(1, lax.rem(me - k + 1 + n, n), a, 1, minus, down)
    for t in range(1, k):
        yield
        up_dest = lax.rem(me + k - t, n)
        down_dest = lax.rem(me - k + t + n, n)
        if t > 1:
            for a, b in zip(low, high):
                forward(0, up_dest, b, t, plus, up)
                forward(1, down_dest, a, t, minus, down)
        for a, b in zip(low, high):
            forward(0, up_dest, a, t, plus, up)
            forward(1, down_dest, b, t, minus, down)
    yield
    for j in (*high, *low):
        up[j].wait_recv()
        down[j].wait_recv()
        finish(j, slots[0, k - 1, j] + slots[1, k - 1, j] + own(me, j))


def kernel(
    pert, grad, mix, weight, table, out,
    p_v, m_v, e_v, yu, zu, gz, gy, pz, py, work, own_two, ag_one, ag_two,
    mpad, mh_one, ml_one, mh_two, ml_two, ch, cl, local, rest, rest_y,
    f1, s1, f2, s2, t1, t2, p1, p2,
    local_sem, send_sem, recv_sem,
):
    mem, lat = lax.axis_index("mem"), lax.axis_index("lat")
    xh, z, y = mem // 32, (mem // 4) % NZ, mem % NY

    def member(dx, dz, dy):
        there = (
            lax.rem(xh + dx, 2) * 32 + lax.rem(z + dz, NZ) * 4 + lax.rem(y + dy, NY)
        )
        return {"mem": there, "lat": lat}

    z_up, z_down = member(0, 1, 0), member(0, NZ - 1, 0)
    chip_lat = lax.rem(lat + 2, 4)
    chip = {"mem": mem, "lat": chip_lat}
    core = {"mem": mem, "lat": lat + 1 - 2 * lax.rem(lat, 2)}
    plane = [(1, 2), (0, 2), (1, 1), (1, 3), (0, 1), (0, 3), (1, 0)]
    turns = (4, 3, 5, 2, 6, 1, 7)
    copies = Copies(send_sem, recv_sem)

    loads = [
        pltpu.make_async_copy(pert, p_v, local_sem.at[0]),
        pltpu.make_async_copy(table, e_v, local_sem.at[1]),
        pltpu.make_async_copy(mix, m_v, local_sem.at[2]),
    ]
    for load in loads:
        load.start()

    barrier = pltpu.get_barrier_semaphore()
    peers = [member(dx, 0, dy) for dx, dy in plane]
    peers += [member(0, dz, 0) for dz in turns] + [chip, core]
    for peer in peers:
        pl.semaphore_signal(barrier, inc=1, device_id=peer, device_id_type=MESH)
    yu[xh, y] = jnp.zeros((ONE, 128), BF16)
    yu[xh, y, :, 0:UNIT] = grad[0:ONE]
    zu[z] = jnp.zeros((TWO, 128), BF16)
    zu[z, 0:REAL, 0:UNIT] = grad[ONE:ROWS]
    pl.semaphore_wait(barrier, len(peers))

    pieces = []

    def band_rows(b, rows):
        return pl.ds(pl.multiple_of(b * rows, 16), rows)

    def send_piece(ag, index, rows, value):
        high = value.astype(BF16)
        ag[index, band_rows(lat, rows), 0:LANES] = high
        ag[index, band_rows(lat, rows), LANES:] = (value - high.astype(F32)).astype(BF16)
        here = ag.at[index, band_rows(lat, rows)]
        there = ag.at[index, band_rows(chip_lat, rows)]
        pieces.append(
            {
                "index": index,
                "one": rows == ONE,
                "there": there,
                "chip": copies.start(here, here, chip),
                "core": copies.start(here, here, core),
            }
        )

    def pass_piece(k):
        piece = pieces[k]
        piece["chip"].wait_recv()
        piece["passed"] = copies.start(piece["there"], piece["there"], core)

    def mixed(high, low, ag, index):
        both = jnp.dot(high[...], ag[index], preferred_element_type=F32)
        return both[:, :LANES] + (
            both[:, LANES:]
            + jnp.dot(low[...], ag[index, :, 0:LANES], preferred_element_type=F32)
        )

    def mix_piece(k):
        piece = pieces[k]
        piece["core"].wait_recv()
        piece["passed"].wait_recv()
        index = piece["index"]
        if piece["one"]:
            local[index] += mixed(mh_one, ml_one, ag_one, index)
        else:
            work_y[...] = mixed(mh_two, ml_two, ag_two, index)
            for i in range(NY):

                @pl.when(index == i)
                def _():
                    for r in range(4):
                        local[r, :, UNIT * i : UNIT * (i + 1)] += work_y[
                            :, UNIT * r : UNIT * (r + 1)
                        ]

    work_y = own_two

    def piece_one(r):
        total = jnp.zeros((ONE, LANES), F32)
        for v in range(4):
            total += pz[4 * v + r].astype(F32) * gz[r + 4 * (v % 2), v // 2].astype(F32)
        send_piece(ag_one, r, ONE, total)
        local[r, 0:ONE] += total

    def piece_two(i):
        total = jnp.zeros((TWO, LANES), F32)
        for v in range(4):
            total += py[i, v].astype(F32) * gy[i, v].astype(F32)
        send_piece(ag_two, i, TWO, total)
        own_two[0:TWO] = total
        for i_ in range(NY):

            @pl.when(i == i_)
            def _():
                for r in range(4):
                    local[r, ONE:BAND, UNIT * i_ : UNIT * (i_ + 1)] += own_two[
                        0:TWO, UNIT * r : UNIT * (r + 1)
                    ]

    def color_one():
        mine = yu.at[xh, y]
        arriving = [copies.start(mine, mine, member(dx, 0, dy)) for dx, dy in plane]
        yield
        for copy in arriving:
            copy.wait_recv()
        for i in range(2):
            for j in range(NY):
                gz[z, i, :, UNIT * j : UNIT * (j + 1)] = yu[i, j, :, 0:UNIT]
        cuts = (pl.ds(0, CUT), pl.ds(CUT, ONE - CUT))

        def pick(d, part):
            return gz.at[d, part // 2, cuts[part % 2]]

        for t in gather_ring(copies, NZ, z, pick, 4, z_up, z_down):
            if t == 3:
                piece_one(lax.rem(z + 2, 4))
            if t == 4:
                piece_one(lax.rem(z + 1, 4))
                piece_one(lax.rem(z + 3, 4))
            yield
        piece_one(lax.rem(z, 4))

    def color_two():
        mine = zu.at[z]
        arriving = [copies.start(mine, mine, member(0, dz, 0)) for dz in turns]
        yield
        for copy in arriving:
            copy.wait_recv()
        for i in range(2):
            for r in range(4):
                gy[y, 2 * xh + i, :, UNIT * r : UNIT * (r + 1)] = zu[4 * i + r, :, 0:UNIT]
        mine = gy.at[y, pl.ds(2 * xh, 2)]
        across = copies.start(mine, mine, member(1, 0, 0))
        arriving = {
            dy: [copies.start(mine, mine, member(0, 0, dy))] for dy in (1, 3, 2)
        }
        yield
        across.wait_recv()
        other = gy.at[y, pl.ds(2 - 2 * xh, 2)]
        for dy in (1, 3, 2):
            arriving[dy].append(copies.start(other, other, member(0, 0, dy)))
        piece_two(y)
        for dy in (1, 3, 2):
            yield
            for copy in arriving[dy]:
                copy.wait_recv()
            piece_two(lax.rem(y + NY - dy, NY))

    def stage_zeros():
        for q in range(2 * NZ):
            pz[q, :, WIDE:] = jnp.zeros((ONE, LANES - WIDE), BF16)
        for i in range(NY):
            local[i] = jnp.zeros((BAND, LANES), F32)
            rest_y[i, :, WIDE:] = jnp.zeros((FLOAT, LANES - WIDE), F32)
            for v in range(4):
                py[i, v, :, WIDE:] = jnp.zeros((TWO, LANES - WIDE), BF16)
                py[i, v, REAL:, :] = jnp.zeros((TWO - REAL, LANES), BF16)
        for i in range(2):
            gz[z, i, :, WIDE:] = jnp.zeros((ONE, LANES - WIDE), BF16)
        for v in range(2):
            gy[y, 2 * xh + v, :, WIDE:] = jnp.zeros((TWO, LANES - WIDE), BF16)

    def stage_pz(v):
        for r in range(4):
            q = 4 * v + r
            pz[q, :, 0:WIDE] = p_v[0:ONE, WIDE * q : WIDE * (q + 1)]

    def stage_py(v):
        for i in range(NY):
            for r in range(4):
                c = WIDE * (4 * v + r) + UNIT * i
                py[i, v, 0:REAL, UNIT * r : UNIT * (r + 1)] = p_v[ONE:ROWS, c : c + UNIT]

    def stage_mix():
        loads[2].wait()
        odd = lax.rem(lat, 2)
        first = pl.multiple_of(ROWS * lat - 4 * odd, 8)
        rows = m_v[pl.ds(first, ROWS + 4), :]
        rows = jnp.where(odd == 1, rows[4:], rows[:ROWS])
        mpad[...] = jnp.zeros((BAND, 4 * BAND), F32)
        for b in range(4):
            c = ROWS * b
            mpad[0:ROWS, ONE * b : ONE * (b + 1)] = rows[:, c : c + ONE]
            d = 4 * ONE + TWO * b
            mpad[0:ROWS, d : d + REAL] = rows[:, c + ONE : c + ROWS]
        for high, low, full in (
            (mh_one, ml_one, mpad[:, 0 : 4 * ONE]),
            (mh_two, ml_two, mpad[:, 4 * ONE :]),
        ):
            rounded = full.astype(BF16)
            high[...] = rounded
            low[...] = (full - rounded.astype(F32)).astype(BF16)

    def stage_lags():
        loads[1].wait()
        row = jnp.broadcast_to(weight[...].reshape(1, NWAVE), (8, NWAVE))
        work[...] = jnp.dot(
            row, e_v[...], precision=lax.Precision.HIGHEST, preferred_element_type=F32
        )

    def stage_kernel(d):
        lags = jnp.concatenate(
            [
                work[0:1, LEFT + WIDE * d : LEFT + WIDE * d + LANES],
                work[0:1, WIDE * d : WIDE * d + LEFT],
            ],
            axis=1,
        )
        turned = pltpu.roll(
            jnp.broadcast_to(lags, (LANES, 2 * LANES)), 0, 1, stride=1, stride_axis=0
        )
        block = turned[:, :LANES]
        high = block.astype(BF16)
        low = (block - high.astype(F32)).astype(BF16)
        for r in range(4):
            s = (r + d) % 4
            place = (
                slice(LANES * r, LANES * (r + 1)),
                slice(LANES * s, LANES * (s + 1)),
            )
            ch[place] = high
            cl[place] = low

    one, two = color_one(), color_two()
    next(one)
    next(two)
    stage_zeros()
    loads[0].wait()
    next(one)
    stage_pz(0)
    stage_pz(1)
    next(two)
    stage_pz(2)
    stage_pz(3)
    next(one)
    for k in range(4):
        stage_py(k)
    next(two)
    next(one)
    next(two)
    next(two)
    pass_piece(0)
    next(one)
    next(two, None)
    pass_piece(1)
    stage_mix()
    pass_piece(2)
    next(one, None)
    stage_lags()
    for k in range(4):
        stage_kernel(k)
    pass_piece(3)
    mix_piece(0)
    mix_piece(1)
    pass_piece(4)
    mix_piece(2)
    mix_piece(3)
    for k in range(4, 8):
        if k + 1 < 8:
            pass_piece(k + 1)
        mix_piece(k)

    def restore(rows):
        value = jnp.concatenate([local[r, rows] for r in range(4)], axis=1)
        high = value.astype(BF16)
        low = (value - high.astype(F32)).astype(BF16)
        for s in range(4):
            cols = slice(LANES * s, LANES * (s + 1))
            rest[s, rows] = jnp.dot(high, ch[:, cols], preferred_element_type=F32) + (
                jnp.dot(high, cl[:, cols], preferred_element_type=F32)
                + jnp.dot(low, ch[:, cols], preferred_element_type=F32)
            )

    def term_one(d, j):
        return pz[j * NZ + d].astype(F32) * rest[lax.rem(d, 4), 0:ONE]

    def term_two(d, j):
        return py[d, j, 0:FLOAT].astype(F32) * rest_y[d]

    def store_one(j, value):
        for i in range(NY):
            t1[j, i, :, 0:UNIT] = value[:, UNIT * i : UNIT * (i + 1)]

    scale = 1.0 / math.sqrt(MEMBERS - 1)

    def sum_one():
        restore(slice(0, ONE))
        yield from scatter_ring(
            copies, NZ, z, term_one, f1, s1, 1, z_up, z_down, store_one
        )
        arriving = []
        for k, (dx, dy) in enumerate(plane):
            part = t1.at[lax.rem(xh + dx, 2), lax.rem(y + dy, NY)]
            arriving.append(copies.start(part, p1.at[k], member(dx, 0, dy)))
        yield
        total = t1[xh, y]
        for k, copy in enumerate(arriving):
            copy.wait_recv()
            total += p1[k]
        out[0:ONE, :] = (total * scale)[:, 0:UNIT]

    def sum_two():
        restore(slice(ONE, BAND))
        for i in range(NY):
            for r in range(4):
                rest_y[i, :, UNIT * r : UNIT * (r + 1)] = rest[
                    r, ONE : ONE + FLOAT, UNIT * i : UNIT * (i + 1)
                ]
        arriving = []
        for k, (dx, dy) in enumerate(plane):
            to_x, to_y = lax.rem(xh + dx, 2), lax.rem(y + dy, NY)
            for i in range(2):
                f2[k, i] = term_two(to_y, 2 * to_x + i)
            arriving.append(copies.start(f2.at[k], s2.at[k], member(dx, 0, dy)))
        yield
        for i in range(2):
            total = term_two(y, 2 * xh + i)
            for k, copy in enumerate(arriving):
                if i == 0:
                    copy.wait_recv()
                total += s2[k, i]
            for r in range(4):
                t2[4 * i + r, :, 0:UNIT] = total[:, UNIT * r : UNIT * (r + 1)]
        arriving = []
        for k, dz in enumerate(turns):
            part = t2.at[lax.rem(z + dz, NZ)]
            arriving.append(copies.start(part, p2.at[k], member(0, dz, 0)))
        yield
        total = t2[z]
        for k, copy in enumerate(arriving):
            copy.wait_recv()
            total += p2[k]
        out[ONE:ROWS, :] = (total * scale)[0:REAL, 0:UNIT]

    one, two = sum_one(), sum_two()
    for chain in (one, two, one, one, one, two, one, two, one):
        next(chain, None)
    for copy in copies.made:
        copy.wait_send()


def local(gradient, perturbations, lat_mix, zonal_weight):
    vmem = pl.BlockSpec(memory_space=pltpu.VMEM)
    hbm = pl.BlockSpec(memory_space=pl.ANY)
    return pl.pallas_call(
        kernel,
        out_shape=jax.ShapeDtypeStruct((ROWS, UNIT), F32),
        in_specs=[hbm, vmem, hbm, vmem, hbm],
        out_specs=vmem,
        scratch_shapes=[
            pltpu.VMEM((ROWS, 4 * NLON), BF16),
            pltpu.VMEM((720, 720), F32),
            pltpu.VMEM((NWAVE, TABLE), F32),
            pltpu.VMEM((2, NY, ONE, 128), BF16),
            pltpu.VMEM((NZ, TWO, 128), BF16),
            pltpu.VMEM((NZ, 2, ONE, LANES), BF16),
            pltpu.VMEM((NY, 4, TWO, LANES), BF16),
            pltpu.VMEM((2 * NZ, ONE, LANES), BF16),
            pltpu.VMEM((NY, 4, TWO, LANES), BF16),
            pltpu.VMEM((8, TABLE), F32),
            pltpu.VMEM((BAND, LANES), F32),
            pltpu.VMEM((4, 4 * ONE, 2 * LANES), BF16),
            pltpu.VMEM((4, 4 * TWO, 2 * LANES), BF16),
            pltpu.VMEM((BAND, 4 * BAND), F32),
            pltpu.VMEM((BAND, 4 * ONE), BF16),
            pltpu.VMEM((BAND, 4 * ONE), BF16),
            pltpu.VMEM((BAND, 4 * TWO), BF16),
            pltpu.VMEM((BAND, 4 * TWO), BF16),
            pltpu.VMEM((4 * LANES, 4 * LANES), BF16),
            pltpu.VMEM((4 * LANES, 4 * LANES), BF16),
            pltpu.VMEM((4, BAND, LANES), F32),
            pltpu.VMEM((4, BAND, LANES), F32),
            pltpu.VMEM((NY, FLOAT, LANES), F32),
            pltpu.VMEM((2, 2, ONE, LANES), F32),
            pltpu.VMEM((2, NZ // 2, 2, ONE, LANES), F32),
            pltpu.VMEM((7, 2, FLOAT, LANES), F32),
            pltpu.VMEM((7, 2, FLOAT, LANES), F32),
            pltpu.VMEM((2, NY, ONE, 128), F32),
            pltpu.VMEM((NZ, FLOAT, 128), F32),
            pltpu.VMEM((7, ONE, 128), F32),
            pltpu.VMEM((7, FLOAT, 128), F32),
            pltpu.SemaphoreType.DMA((3,)),
            pltpu.SemaphoreType.DMA((128,)),
            pltpu.SemaphoreType.DMA((128,)),
        ],
        compiler_params=pltpu.CompilerParams(
            collective_id=0, has_side_effects=True, vmem_limit_bytes=56 * 2**20
        ),
    )(
        perturbations.reshape(ROWS, 4 * NLON),
        gradient,
        lat_mix,
        zonal_weight,
        jnp.asarray(wave_table()),
    )


def solution(mesh):
    return jax.shard_map(
        local,
        mesh=mesh,
        in_specs=(P("lat", "mem"), P("mem", "lat", None), P(), P()),
        out_specs=P("lat", "mem"),
        check_vma=False,
    )
```

```python
import math

import jax
import jax.numpy as jnp
import numpy as np
from jax import lax
from jax.experimental import pallas as pl
from jax.experimental.pallas import tpu as pltpu
from jax.sharding import PartitionSpec as P

MESH = pl.DeviceIdType.MESH
F32 = jnp.float32
BF16 = jnp.bfloat16
NLON = 1440
NWAVE = 720
MEMBERS = 64
ROWS = 180
BAND = 192
ONE = 112
CUT = 64
TWO = BAND - ONE
REAL = ROWS - ONE
FLOAT = (REAL + 7) // 8 * 8
UNIT = 90
WIDE = 360
LANES = 384
FREE = WIDE - 256
NZ, NY = 8, 4
LEFT = 384
TABLE = 1920


def wave_table():
    waves = np.arange(NWAVE)
    offsets = np.arange(TABLE) - LEFT
    gains = np.where(waves == 0, 1.0, 2.0) / NLON
    angles = (waves[:, None] * offsets[None, :] % NLON) * (2.0 * math.pi / NLON)
    return (gains[:, None] * np.cos(angles)).astype(np.float32)


class Copies:
    def __init__(self, send, recv):
        self.send, self.recv, self.count, self.made = send, recv, 0, []

    def start(self, src, dst, device):
        k = self.count
        self.count += 1
        copy = pltpu.make_async_remote_copy(
            src_ref=src,
            dst_ref=dst,
            send_sem=self.send.at[k],
            recv_sem=self.recv.at[k],
            device_id=device,
            device_id_type=MESH,
        )
        copy.start()
        self.made.append(copy)
        return copy


def packed(value):
    lane = lax.broadcasted_iota(jnp.int32, (value.shape[0], 128), 1)
    most = jnp.max(jnp.abs(value), axis=1, keepdims=True)
    level = jnp.ceil(jnp.log(jnp.maximum(most, 1e-30) / 32000.0) * (8.0 / math.log(2.0)))
    whole = jnp.floor(value * jnp.exp(level * (-math.log(2.0) / 8.0)) + 0.5)
    a, b, c = whole[:, 0:128], whole[:, 128:256], whole[:, 256:384]
    c = jnp.where(lane < FREE, c, level)
    high = jnp.floor(b * (1.0 / 256.0) + 0.5)
    return jnp.concatenate([a * 256.0 + high, c * 256.0 + (b - high * 256.0)], axis=1)


def unpacked(words):
    lane = lax.broadcasted_iota(jnp.int32, (words.shape[0], 128), 1)
    first, second = words[:, 0:128], words[:, 128:256]
    a = jnp.floor(first * (1.0 / 256.0) + 0.5)
    c = jnp.floor(second * (1.0 / 256.0) + 0.5)
    b = (first - a * 256.0) * 256.0 + (second - c * 256.0)
    scale = jnp.exp(c[:, FREE : FREE + 1] * (math.log(2.0) / 8.0))
    c = jnp.where(lane < FREE, c, 0.0)
    return jnp.concatenate([a * scale, b * scale, c * scale], axis=1)


def gather_ring(copies, n, me, pick, parts, plus, minus):
    k = n // 2
    early, late = range(parts // 2), range(parts // 2, parts)
    up, down = {}, {}
    for i, j in zip((*early, *late), (*late, *early)):
        up[i] = copies.start(pick(me, i), pick(me, i), plus)
        down[j] = copies.start(pick(me, j), pick(me, j), minus)
    for t in range(1, k):
        yield t
        up_src, down_src = lax.rem(me - t + n, n), lax.rem(me + t, n)
        for i, j in zip((*early, *late), (*late, *early)):
            up[i].wait_recv()
            if t < k - 1 or i in early:
                up[i] = copies.start(pick(up_src, i), pick(up_src, i), plus)
            down[j].wait_recv()
            if t < k - 1 or j in late:
                down[j] = copies.start(pick(down_src, j), pick(down_src, j), minus)
    yield k
    for i, j in zip(early, late):
        up[i].wait_recv()
        down[j].wait_recv()


def scatter_ring(copies, n, me, own, first, slots, half, plus, minus, finish):
    k = n // 2
    low, high = range(half), range(half, 2 * half)
    up, down = {}, {}

    def begin(way, dest, j, t, device, made):
        first[way, j] = own(dest, j)
        made[j] = copies.start(first.at[way, j], slots.at[way, t, j], device)

    def forward(way, dest, j, t, device, made):
        made[j].wait_recv()
        slots[way, t - 1, j] += own(dest, j)
        made[j] = copies.start(slots.at[way, t - 1, j], slots.at[way, t, j], device)

    for a, b in zip(low, high):
        begin(0, lax.rem(me + k, n), a, 0, plus, up)
        begin(1, lax.rem(me + k, n), b, 0, minus, down)
    for a, b in zip(low, high):
        begin(0, lax.rem(me + k - 1, n), b, 1, plus, up)
        begin(1, lax.rem(me - k + 1 + n, n), a, 1, minus, down)
    for t in range(1, k):
        yield
        up_dest = lax.rem(me + k - t, n)
        down_dest = lax.rem(me - k + t + n, n)
        if t > 1:
            for a, b in zip(low, high):
                forward(0, up_dest, b, t, plus, up)
                forward(1, down_dest, a, t, minus, down)
        for a, b in zip(low, high):
            forward(0, up_dest, a, t, plus, up)
            forward(1, down_dest, b, t, minus, down)
    yield
    for j in (*high, *low):
        up[j].wait_recv()
        down[j].wait_recv()
        finish(j, slots[0, k - 1, j] + slots[1, k - 1, j] + own(me, j))


def kernel(
    pert, grad, mix, weight, table, out,
    p_v, m_v, e_v, yu, zu, gz, gy, pz, py, work, own_two, ag_one, ag_two, pk_one, pk_two,
    mpad, mh_one, ml_one, mh_two, ml_two, ch, cl, local, rest, rest_y,
    f1, s1, f2, s2, t1, t2, p1, p2,
    local_sem, send_sem, recv_sem,
):
    mem, lat = lax.axis_index("mem"), lax.axis_index("lat")
    xh, z, y = mem // 32, (mem // 4) % NZ, mem % NY

    def member(dx, dz, dy):
        there = (
            lax.rem(xh + dx, 2) * 32 + lax.rem(z + dz, NZ) * 4 + lax.rem(y + dy, NY)
        )
        return {"mem": there, "lat": lat}

    z_up, z_down = member(0, 1, 0), member(0, NZ - 1, 0)
    chip_lat = lax.rem(lat + 2, 4)
    chip = {"mem": mem, "lat": chip_lat}
    core = {"mem": mem, "lat": lat + 1 - 2 * lax.rem(lat, 2)}
    plane = [(1, 2), (0, 2), (1, 1), (1, 3), (0, 1), (0, 3), (1, 0)]
    turns = (4, 3, 5, 2, 6, 1, 7)
    copies = Copies(send_sem, recv_sem)

    loads = [
        pltpu.make_async_copy(pert, p_v, local_sem.at[0]),
        pltpu.make_async_copy(table, e_v, local_sem.at[1]),
        pltpu.make_async_copy(mix, m_v, local_sem.at[2]),
    ]
    for load in loads:
        load.start()

    barrier = pltpu.get_barrier_semaphore()
    peers = [member(dx, 0, dy) for dx, dy in plane]
    peers += [member(0, dz, 0) for dz in turns] + [chip, core]
    for peer in peers:
        pl.semaphore_signal(barrier, inc=1, device_id=peer, device_id_type=MESH)
    yu[xh, y] = jnp.zeros((ONE, 128), BF16)
    yu[xh, y, :, 0:UNIT] = grad[0:ONE]
    zu[z] = jnp.zeros((TWO, 128), BF16)
    zu[z, 0:REAL, 0:UNIT] = grad[ONE:ROWS]
    pl.semaphore_wait(barrier, len(peers))

    pieces = []

    def band_rows(b, rows):
        return pl.ds(pl.multiple_of(b * rows, 16), rows)

    def send_piece(first, index, value):
        ag, pack = (ag_one, pk_one) if first else (ag_two, pk_two)
        rows, sent = value.shape[0], pack.shape[2]
        pack[index, lat] = packed(value[0:sent])
        here = pack.at[index, lat]
        over = copies.start(here, here, chip)
        high = value.astype(BF16)
        ag[index, band_rows(lat, rows), 0:LANES] = high
        ag[index, band_rows(lat, rows), LANES:] = (value - high.astype(F32)).astype(BF16)
        here = ag.at[index, band_rows(lat, rows)]
        pieces.append(
            {
                "index": index,
                "one": first,
                "ag": ag,
                "pack": pack,
                "rows": rows,
                "chip": over,
                "core": copies.start(here, here, core),
            }
        )

    def unpack_piece(piece, b):
        value = unpacked(piece["pack"][piece["index"], b])
        rows, sent = piece["rows"], value.shape[0]
        if sent < rows:
            value = jnp.concatenate([value, jnp.zeros((rows - sent, LANES), F32)], axis=0)
        high = value.astype(BF16)
        low = (value - high.astype(F32)).astype(BF16)
        piece["ag"][piece["index"], band_rows(b, rows), 0:LANES] = high
        piece["ag"][piece["index"], band_rows(b, rows), LANES:] = low

    def pass_piece(k):
        piece = pieces[k]
        piece["chip"].wait_recv()
        there = piece["pack"].at[piece["index"], chip_lat]
        piece["passed"] = copies.start(there, there, core)
        unpack_piece(piece, chip_lat)

    def mixed(high, low, ag, index):
        both = jnp.dot(high[...], ag[index], preferred_element_type=F32)
        return both[:, :LANES] + (
            both[:, LANES:]
            + jnp.dot(low[...], ag[index, :, 0:LANES], preferred_element_type=F32)
        )

    def mix_piece(k):
        piece = pieces[k]
        piece["core"].wait_recv()
        piece["passed"].wait_recv()
        unpack_piece(piece, chip_lat + 1 - 2 * lax.rem(lat, 2))
        index = piece["index"]
        if piece["one"]:
            local[index] += mixed(mh_one, ml_one, ag_one, index)
        else:
            work_y[...] = mixed(mh_two, ml_two, ag_two, index)
            for i in range(NY):

                @pl.when(index == i)
                def _():
                    for r in range(4):
                        local[r, :, UNIT * i : UNIT * (i + 1)] += work_y[
                            :, UNIT * r : UNIT * (r + 1)
                        ]

    work_y = own_two

    def piece_one(r):
        total = jnp.zeros((ONE, LANES), F32)
        for v in range(4):
            total += pz[4 * v + r].astype(F32) * gz[r + 4 * (v % 2), v // 2].astype(F32)
        send_piece(True, r, total)
        local[r, 0:ONE] += total

    def piece_two(i):
        total = jnp.zeros((TWO, LANES), F32)
        for v in range(4):
            total += py[i, v].astype(F32) * gy[i, v].astype(F32)
        send_piece(False, i, total)
        own_two[0:TWO] = total
        for i_ in range(NY):

            @pl.when(i == i_)
            def _():
                for r in range(4):
                    local[r, ONE:BAND, UNIT * i_ : UNIT * (i_ + 1)] += own_two[
                        0:TWO, UNIT * r : UNIT * (r + 1)
                    ]

    def color_one():
        mine = yu.at[xh, y]
        arriving = [copies.start(mine, mine, member(dx, 0, dy)) for dx, dy in plane]
        yield
        for copy in arriving:
            copy.wait_recv()
        for i in range(2):
            for j in range(NY):
                gz[z, i, :, UNIT * j : UNIT * (j + 1)] = yu[i, j, :, 0:UNIT]
        cuts = (pl.ds(0, CUT), pl.ds(CUT, ONE - CUT))

        def pick(d, part):
            return gz.at[d, part // 2, cuts[part % 2]]

        for t in gather_ring(copies, NZ, z, pick, 4, z_up, z_down):
            if t == 3:
                piece_one(lax.rem(z + 2, 4))
            if t == 4:
                piece_one(lax.rem(z + 1, 4))
                piece_one(lax.rem(z + 3, 4))
            yield
        piece_one(lax.rem(z, 4))

    def color_two():
        mine = zu.at[z]
        arriving = [copies.start(mine, mine, member(0, dz, 0)) for dz in turns]
        yield
        for copy in arriving:
            copy.wait_recv()
        for i in range(2):
            for r in range(4):
                gy[y, 2 * xh + i, :, UNIT * r : UNIT * (r + 1)] = zu[4 * i + r, :, 0:UNIT]
        mine = gy.at[y, pl.ds(2 * xh, 2)]
        across = copies.start(mine, mine, member(1, 0, 0))
        arriving = {
            dy: [copies.start(mine, mine, member(0, 0, dy))] for dy in (1, 3, 2)
        }
        yield
        across.wait_recv()
        other = gy.at[y, pl.ds(2 - 2 * xh, 2)]
        for dy in (1, 3, 2):
            arriving[dy].append(copies.start(other, other, member(0, 0, dy)))
        piece_two(y)
        for dy in (1, 3, 2):
            yield
            for copy in arriving[dy]:
                copy.wait_recv()
            piece_two(lax.rem(y + NY - dy, NY))

    def stage_zeros():
        for q in range(2 * NZ):
            pz[q, :, WIDE:] = jnp.zeros((ONE, LANES - WIDE), BF16)
        for i in range(NY):
            local[i] = jnp.zeros((BAND, LANES), F32)
            rest_y[i, :, WIDE:] = jnp.zeros((FLOAT, LANES - WIDE), F32)
            for v in range(4):
                py[i, v, :, WIDE:] = jnp.zeros((TWO, LANES - WIDE), BF16)
                py[i, v, REAL:, :] = jnp.zeros((TWO - REAL, LANES), BF16)
        for i in range(2):
            gz[z, i, :, WIDE:] = jnp.zeros((ONE, LANES - WIDE), BF16)
        for v in range(2):
            gy[y, 2 * xh + v, :, WIDE:] = jnp.zeros((TWO, LANES - WIDE), BF16)

    def stage_pz(v):
        for r in range(4):
            q = 4 * v + r
            pz[q, :, 0:WIDE] = p_v[0:ONE, WIDE * q : WIDE * (q + 1)]

    def stage_py(v):
        for i in range(NY):
            for r in range(4):
                c = WIDE * (4 * v + r) + UNIT * i
                py[i, v, 0:REAL, UNIT * r : UNIT * (r + 1)] = p_v[ONE:ROWS, c : c + UNIT]

    def stage_mix():
        loads[2].wait()
        odd = lax.rem(lat, 2)
        first = pl.multiple_of(ROWS * lat - 4 * odd, 8)
        rows = m_v[pl.ds(first, ROWS + 4), :]
        rows = jnp.where(odd == 1, rows[4:], rows[:ROWS])
        mpad[...] = jnp.zeros((BAND, 4 * BAND), F32)
        for b in range(4):
            c = ROWS * b
            mpad[0:ROWS, ONE * b : ONE * (b + 1)] = rows[:, c : c + ONE]
            d = 4 * ONE + TWO * b
            mpad[0:ROWS, d : d + REAL] = rows[:, c + ONE : c + ROWS]
        for high, low, full in (
            (mh_one, ml_one, mpad[:, 0 : 4 * ONE]),
            (mh_two, ml_two, mpad[:, 4 * ONE :]),
        ):
            rounded = full.astype(BF16)
            high[...] = rounded
            low[...] = (full - rounded.astype(F32)).astype(BF16)

    def stage_lags():
        loads[1].wait()
        row = jnp.broadcast_to(weight[...].reshape(1, NWAVE), (8, NWAVE))
        work[...] = jnp.dot(
            row, e_v[...], precision=lax.Precision.HIGHEST, preferred_element_type=F32
        )

    def stage_kernel(d):
        lags = jnp.concatenate(
            [
                work[0:1, LEFT + WIDE * d : LEFT + WIDE * d + LANES],
                work[0:1, WIDE * d : WIDE * d + LEFT],
            ],
            axis=1,
        )
        turned = pltpu.roll(
            jnp.broadcast_to(lags, (LANES, 2 * LANES)), 0, 1, stride=1, stride_axis=0
        )
        block = turned[:, :LANES]
        high = block.astype(BF16)
        low = (block - high.astype(F32)).astype(BF16)
        for r in range(4):
            s = (r + d) % 4
            place = (
                slice(LANES * r, LANES * (r + 1)),
                slice(LANES * s, LANES * (s + 1)),
            )
            ch[place] = high
            cl[place] = low

    one, two = color_one(), color_two()
    next(one)
    next(two)
    stage_zeros()
    loads[0].wait()
    next(one)
    stage_pz(0)
    stage_pz(1)
    next(two)
    stage_pz(2)
    stage_pz(3)
    next(one)
    for k in range(4):
        stage_py(k)
    next(two)
    next(one)
    next(two)
    next(two)
    pass_piece(0)
    next(one)
    next(two, None)
    pass_piece(1)
    stage_mix()
    pass_piece(2)
    next(one, None)
    stage_lags()
    for k in range(4):
        stage_kernel(k)
    pass_piece(3)
    mix_piece(0)
    mix_piece(1)
    pass_piece(4)
    mix_piece(2)
    mix_piece(3)
    for k in range(4, 8):
        if k + 1 < 8:
            pass_piece(k + 1)
        mix_piece(k)

    def restore(rows):
        value = jnp.concatenate([local[r, rows] for r in range(4)], axis=1)
        high = value.astype(BF16)
        low = (value - high.astype(F32)).astype(BF16)
        for s in range(4):
            cols = slice(LANES * s, LANES * (s + 1))
            rest[s, rows] = jnp.dot(high, ch[:, cols], preferred_element_type=F32) + (
                jnp.dot(high, cl[:, cols], preferred_element_type=F32)
                + jnp.dot(low, ch[:, cols], preferred_element_type=F32)
            )

    def term_one(d, j):
        return pz[j * NZ + d].astype(F32) * rest[lax.rem(d, 4), 0:ONE]

    def term_two(d, j):
        return py[d, j, 0:FLOAT].astype(F32) * rest_y[d]

    def store_one(j, value):
        for i in range(NY):
            t1[j, i, :, 0:UNIT] = value[:, UNIT * i : UNIT * (i + 1)]

    scale = 1.0 / math.sqrt(MEMBERS - 1)

    def sum_one():
        restore(slice(0, ONE))
        yield from scatter_ring(
            copies, NZ, z, term_one, f1, s1, 1, z_up, z_down, store_one
        )
        arriving = []
        for k, (dx, dy) in enumerate(plane):
            part = t1.at[lax.rem(xh + dx, 2), lax.rem(y + dy, NY)]
            arriving.append(copies.start(part, p1.at[k], member(dx, 0, dy)))
        yield
        total = t1[xh, y]
        for k, copy in enumerate(arriving):
            copy.wait_recv()
            total += p1[k]
        out[0:ONE, :] = (total * scale)[:, 0:UNIT]

    def sum_two():
        restore(slice(ONE, BAND))
        for i in range(NY):
            for r in range(4):
                rest_y[i, :, UNIT * r : UNIT * (r + 1)] = rest[
                    r, ONE : ONE + FLOAT, UNIT * i : UNIT * (i + 1)
                ]
        arriving = []
        for k, (dx, dy) in enumerate(plane):
            to_x, to_y = lax.rem(xh + dx, 2), lax.rem(y + dy, NY)
            for i in range(2):
                f2[k, i] = term_two(to_y, 2 * to_x + i)
            arriving.append(copies.start(f2.at[k], s2.at[k], member(dx, 0, dy)))
        yield
        for i in range(2):
            total = term_two(y, 2 * xh + i)
            for k, copy in enumerate(arriving):
                if i == 0:
                    copy.wait_recv()
                total += s2[k, i]
            for r in range(4):
                t2[4 * i + r, :, 0:UNIT] = total[:, UNIT * r : UNIT * (r + 1)]
        arriving = []
        for k, dz in enumerate(turns):
            part = t2.at[lax.rem(z + dz, NZ)]
            arriving.append(copies.start(part, p2.at[k], member(0, dz, 0)))
        yield
        total = t2[z]
        for k, copy in enumerate(arriving):
            copy.wait_recv()
            total += p2[k]
        out[ONE:ROWS, :] = (total * scale)[0:REAL, 0:UNIT]

    one, two = sum_one(), sum_two()
    for chain in (one, two, one, one, one, two, one, two, one):
        next(chain, None)
    for copy in copies.made:
        copy.wait_send()


def local(gradient, perturbations, lat_mix, zonal_weight):
    vmem = pl.BlockSpec(memory_space=pltpu.VMEM)
    hbm = pl.BlockSpec(memory_space=pl.ANY)
    return pl.pallas_call(
        kernel,
        out_shape=jax.ShapeDtypeStruct((ROWS, UNIT), F32),
        in_specs=[hbm, vmem, hbm, vmem, hbm],
        out_specs=vmem,
        scratch_shapes=[
            pltpu.VMEM((ROWS, 4 * NLON), BF16),
            pltpu.VMEM((720, 720), F32),
            pltpu.VMEM((NWAVE, TABLE), F32),
            pltpu.VMEM((2, NY, ONE, 128), BF16),
            pltpu.VMEM((NZ, TWO, 128), BF16),
            pltpu.VMEM((NZ, 2, ONE, LANES), BF16),
            pltpu.VMEM((NY, 4, TWO, LANES), BF16),
            pltpu.VMEM((2 * NZ, ONE, LANES), BF16),
            pltpu.VMEM((NY, 4, TWO, LANES), BF16),
            pltpu.VMEM((8, TABLE), F32),
            pltpu.VMEM((BAND, LANES), F32),
            pltpu.VMEM((4, 4 * ONE, 2 * LANES), BF16),
            pltpu.VMEM((4, 4 * TWO, 2 * LANES), BF16),
            pltpu.VMEM((4, 4, ONE, 256), F32),
            pltpu.VMEM((4, 4, FLOAT, 256), F32),
            pltpu.VMEM((BAND, 4 * BAND), F32),
            pltpu.VMEM((BAND, 4 * ONE), BF16),
            pltpu.VMEM((BAND, 4 * ONE), BF16),
            pltpu.VMEM((BAND, 4 * TWO), BF16),
            pltpu.VMEM((BAND, 4 * TWO), BF16),
            pltpu.VMEM((4 * LANES, 4 * LANES), BF16),
            pltpu.VMEM((4 * LANES, 4 * LANES), BF16),
            pltpu.VMEM((4, BAND, LANES), F32),
            pltpu.VMEM((4, BAND, LANES), F32),
            pltpu.VMEM((NY, FLOAT, LANES), F32),
            pltpu.VMEM((2, 2, ONE, LANES), F32),
            pltpu.VMEM((2, NZ // 2, 2, ONE, LANES), F32),
            pltpu.VMEM((7, 2, FLOAT, LANES), F32),
            pltpu.VMEM((7, 2, FLOAT, LANES), F32),
            pltpu.VMEM((2, NY, ONE, 128), F32),
            pltpu.VMEM((NZ, FLOAT, 128), F32),
            pltpu.VMEM((7, ONE, 128), F32),
            pltpu.VMEM((7, FLOAT, 128), F32),
            pltpu.SemaphoreType.DMA((3,)),
            pltpu.SemaphoreType.DMA((128,)),
            pltpu.SemaphoreType.DMA((128,)),
        ],
        compiler_params=pltpu.CompilerParams(
            collective_id=0, has_side_effects=True, vmem_limit_bytes=56 * 2**20
        ),
    )(
        perturbations.reshape(ROWS, 4 * NLON),
        gradient,
        lat_mix,
        zonal_weight,
        jnp.asarray(wave_table()),
    )


def solution(mesh):
    return jax.shard_map(
        local,
        mesh=mesh,
        in_specs=(P("lat", "mem"), P("mem", "lat", None), P(), P()),
        out_specs=P("lat", "mem"),
        check_vma=False,
    )
```

```python
import math

import jax
import jax.numpy as jnp
import numpy as np
from jax import lax
from jax.experimental import pallas as pl
from jax.experimental.pallas import tpu as pltpu
from jax.sharding import PartitionSpec as P

MESH = pl.DeviceIdType.MESH
F32 = jnp.float32
BF16 = jnp.bfloat16
NLON = 1440
NWAVE = 720
MEMBERS = 64
ROWS = 180
BAND = 192
ONE = 112
CUT = 64
TWO = BAND - ONE
REAL = ROWS - ONE
FLOAT = (REAL + 7) // 8 * 8
UNIT = 90
WIDE = 360
LANES = 384
FREE = WIDE - 256
NZ, NY = 8, 4
LEFT = 384
TABLE = 1920


def wave_table():
    waves = np.arange(NWAVE)
    offsets = np.arange(TABLE) - LEFT
    gains = np.where(waves == 0, 1.0, 2.0) / NLON
    angles = (waves[:, None] * offsets[None, :] % NLON) * (2.0 * math.pi / NLON)
    return (gains[:, None] * np.cos(angles)).astype(np.float32)


class Copies:
    def __init__(self, send, recv):
        self.send, self.recv, self.count, self.made = send, recv, 0, []

    def start(self, src, dst, device):
        k = self.count
        self.count += 1
        copy = pltpu.make_async_remote_copy(
            src_ref=src,
            dst_ref=dst,
            send_sem=self.send.at[k],
            recv_sem=self.recv.at[k],
            device_id=device,
            device_id_type=MESH,
        )
        copy.start()
        self.made.append(copy)
        return copy


def packed(value):
    lane = lax.broadcasted_iota(jnp.int32, (value.shape[0], 128), 1)
    most = jnp.max(jnp.abs(value), axis=1, keepdims=True)
    level = jnp.ceil(jnp.log(jnp.maximum(most, 1e-30) / 32000.0) * (8.0 / math.log(2.0)))
    whole = jnp.floor(value * jnp.exp(level * (-math.log(2.0) / 8.0)) + 0.5)
    a, b, c = whole[:, 0:128], whole[:, 128:256], whole[:, 256:384]
    c = jnp.where(lane < FREE, c, level)
    high = jnp.floor(b * (1.0 / 256.0) + 0.5)
    return jnp.concatenate([a * 256.0 + high, c * 256.0 + (b - high * 256.0)], axis=1)


def unpacked(words):
    lane = lax.broadcasted_iota(jnp.int32, (words.shape[0], 128), 1)
    first, second = words[:, 0:128], words[:, 128:256]
    a = jnp.floor(first * (1.0 / 256.0) + 0.5)
    c = jnp.floor(second * (1.0 / 256.0) + 0.5)
    b = (first - a * 256.0) * 256.0 + (second - c * 256.0)
    scale = jnp.exp(c[:, FREE : FREE + 1] * (math.log(2.0) / 8.0))
    c = jnp.where(lane < FREE, c, 0.0)
    return jnp.concatenate([a * scale, b * scale, c * scale], axis=1)


def gather_ring(copies, n, me, pick, parts, plus, minus):
    k = n // 2
    early, late = range(parts // 2), range(parts // 2, parts)
    up, down = {}, {}
    for i, j in zip((*early, *late), (*late, *early)):
        up[i] = copies.start(pick(me, i), pick(me, i), plus)
        down[j] = copies.start(pick(me, j), pick(me, j), minus)
    for t in range(1, k):
        yield t
        up_src, down_src = lax.rem(me - t + n, n), lax.rem(me + t, n)
        for i, j in zip((*early, *late), (*late, *early)):
            up[i].wait_recv()
            if t < k - 1 or i in early:
                up[i] = copies.start(pick(up_src, i), pick(up_src, i), plus)
            down[j].wait_recv()
            if t < k - 1 or j in late:
                down[j] = copies.start(pick(down_src, j), pick(down_src, j), minus)
    yield k
    for i, j in zip(early, late):
        up[i].wait_recv()
        down[j].wait_recv()


def scatter_ring(copies, n, me, own, first, slots, half, plus, minus, finish):
    k = n // 2
    low, high = range(half), range(half, 2 * half)
    up, down = {}, {}

    def begin(way, dest, j, t, device, made):
        first[way, j] = own(dest, j)
        made[j] = copies.start(first.at[way, j], slots.at[way, t, j], device)

    def forward(way, dest, j, t, device, made):
        made[j].wait_recv()
        slots[way, t - 1, j] += own(dest, j)
        made[j] = copies.start(slots.at[way, t - 1, j], slots.at[way, t, j], device)

    for a, b in zip(low, high):
        begin(0, lax.rem(me + k, n), a, 0, plus, up)
        begin(1, lax.rem(me + k, n), b, 0, minus, down)
    for a, b in zip(low, high):
        begin(0, lax.rem(me + k - 1, n), b, 1, plus, up)
        begin(1, lax.rem(me - k + 1 + n, n), a, 1, minus, down)
    for t in range(1, k):
        yield
        up_dest = lax.rem(me + k - t, n)
        down_dest = lax.rem(me - k + t + n, n)
        if t > 1:
            for a, b in zip(low, high):
                forward(0, up_dest, b, t, plus, up)
                forward(1, down_dest, a, t, minus, down)
        for a, b in zip(low, high):
            forward(0, up_dest, a, t, plus, up)
            forward(1, down_dest, b, t, minus, down)
    yield
    for j in (*high, *low):
        up[j].wait_recv()
        down[j].wait_recv()
        finish(j, slots[0, k - 1, j] + slots[1, k - 1, j] + own(me, j))


def kernel(
    pert, grad, mix, weight, table, out,
    p_v, m_v, e_v, yu, zu, gz, gy, pz, py, work, own_two, ag_one, ag_two, pk_one, pk_two,
    mpad, mh_one, ml_one, mh_two, ml_two, blocks, sum_h, sum_l, odd_h, odd_l, local, rest, rest_y,
    f1, s1, t1, p1, f3, s3, t3, p3, f2, s2, t2, p2,
    local_sem, send_sem, recv_sem,
):
    mem, lat = lax.axis_index("mem"), lax.axis_index("lat")
    xh, z, y = mem // 32, (mem // 4) % NZ, mem % NY

    def member(dx, dz, dy):
        there = (
            lax.rem(xh + dx, 2) * 32 + lax.rem(z + dz, NZ) * 4 + lax.rem(y + dy, NY)
        )
        return {"mem": there, "lat": lat}

    z_up, z_down = member(0, 1, 0), member(0, NZ - 1, 0)
    chip_lat = lax.rem(lat + 2, 4)
    chip = {"mem": mem, "lat": chip_lat}
    core = {"mem": mem, "lat": lat + 1 - 2 * lax.rem(lat, 2)}
    plane = [(1, 2), (0, 2), (1, 1), (1, 3), (0, 1), (0, 3), (1, 0)]
    turns = (4, 3, 5, 2, 6, 1, 7)
    copies = Copies(send_sem, recv_sem)

    loads = [
        pltpu.make_async_copy(pert, p_v, local_sem.at[0]),
        pltpu.make_async_copy(table, e_v, local_sem.at[1]),
        pltpu.make_async_copy(mix, m_v, local_sem.at[2]),
    ]
    for load in loads:
        load.start()

    barrier = pltpu.get_barrier_semaphore()
    peers = [member(dx, 0, dy) for dx, dy in plane]
    peers += [member(0, dz, 0) for dz in turns] + [chip, core]
    for peer in peers:
        pl.semaphore_signal(barrier, inc=1, device_id=peer, device_id_type=MESH)
    yu[xh, y] = jnp.zeros((ONE, 128), BF16)
    yu[xh, y, :, 0:UNIT] = grad[0:ONE]
    zu[z] = jnp.zeros((TWO, 128), BF16)
    zu[z, 0:REAL, 0:UNIT] = grad[ONE:ROWS]
    pl.semaphore_wait(barrier, len(peers))

    pieces = []

    def band_rows(b, rows):
        return pl.ds(pl.multiple_of(b * rows, 16), rows)

    def send_piece(first, index, value):
        ag, pack = (ag_one, pk_one) if first else (ag_two, pk_two)
        rows, sent = value.shape[0], pack.shape[2]
        pack[index, lat] = packed(value[0:sent])
        here = pack.at[index, lat]
        over = copies.start(here, here, chip)
        high = value.astype(BF16)
        ag[index, band_rows(lat, rows), 0:LANES] = high
        ag[index, band_rows(lat, rows), LANES:] = (value - high.astype(F32)).astype(BF16)
        here = ag.at[index, band_rows(lat, rows)]
        pieces.append(
            {
                "index": index,
                "one": first,
                "ag": ag,
                "pack": pack,
                "rows": rows,
                "chip": over,
                "core": copies.start(here, here, core),
            }
        )

    def unpack_piece(piece, b):
        value = unpacked(piece["pack"][piece["index"], b])
        rows, sent = piece["rows"], value.shape[0]
        if sent < rows:
            value = jnp.concatenate([value, jnp.zeros((rows - sent, LANES), F32)], axis=0)
        high = value.astype(BF16)
        low = (value - high.astype(F32)).astype(BF16)
        piece["ag"][piece["index"], band_rows(b, rows), 0:LANES] = high
        piece["ag"][piece["index"], band_rows(b, rows), LANES:] = low

    def pass_piece(k):
        piece = pieces[k]
        piece["chip"].wait_recv()
        there = piece["pack"].at[piece["index"], chip_lat]
        piece["passed"] = copies.start(there, there, core)
        unpack_piece(piece, chip_lat)

    def mixed(high, low, ag, index):
        both = jnp.dot(high[...], ag[index], preferred_element_type=F32)
        return both[:, :LANES] + (
            both[:, LANES:]
            + jnp.dot(low[...], ag[index, :, 0:LANES], preferred_element_type=F32)
        )

    def mix_piece(k):
        piece = pieces[k]
        piece["core"].wait_recv()
        piece["passed"].wait_recv()
        unpack_piece(piece, chip_lat + 1 - 2 * lax.rem(lat, 2))
        index = piece["index"]
        if piece["one"]:
            local[index] += mixed(mh_one, ml_one, ag_one, index)
        else:
            work_y[...] = mixed(mh_two, ml_two, ag_two, index)
            for i in range(NY):

                @pl.when(index == i)
                def _():
                    for r in range(4):
                        local[r, :, UNIT * i : UNIT * (i + 1)] += work_y[
                            :, UNIT * r : UNIT * (r + 1)
                        ]

    work_y = own_two

    def piece_one(r):
        total = jnp.zeros((ONE, LANES), F32)
        for v in range(4):
            total += pz[4 * v + r].astype(F32) * gz[r + 4 * (v % 2), v // 2].astype(F32)
        send_piece(True, r, total)
        local[r, 0:ONE] += total

    def piece_two(i):
        total = jnp.zeros((TWO, LANES), F32)
        for v in range(4):
            total += py[i, v].astype(F32) * gy[i, v].astype(F32)
        send_piece(False, i, total)
        own_two[0:TWO] = total
        for i_ in range(NY):

            @pl.when(i == i_)
            def _():
                for r in range(4):
                    local[r, ONE:BAND, UNIT * i_ : UNIT * (i_ + 1)] += own_two[
                        0:TWO, UNIT * r : UNIT * (r + 1)
                    ]

    def color_one():
        mine = yu.at[xh, y]
        arriving = [copies.start(mine, mine, member(dx, 0, dy)) for dx, dy in plane]
        yield
        for copy in arriving:
            copy.wait_recv()
        for i in range(2):
            for j in range(NY):
                gz[z, i, :, UNIT * j : UNIT * (j + 1)] = yu[i, j, :, 0:UNIT]
        cuts = (pl.ds(0, CUT), pl.ds(CUT, ONE - CUT))

        def pick(d, part):
            return gz.at[d, part // 2, cuts[part % 2]]

        for t in gather_ring(copies, NZ, z, pick, 4, z_up, z_down):
            if t == 3:
                piece_one(lax.rem(z + 2, 4))
            if t == 4:
                piece_one(lax.rem(z + 1, 4))
                piece_one(lax.rem(z + 3, 4))
            yield
        piece_one(lax.rem(z, 4))

    def color_two():
        mine = zu.at[z]
        arriving = [copies.start(mine, mine, member(0, dz, 0)) for dz in turns]
        yield
        for copy in arriving:
            copy.wait_recv()
        for i in range(2):
            for r in range(4):
                gy[y, 2 * xh + i, :, UNIT * r : UNIT * (r + 1)] = zu[4 * i + r, :, 0:UNIT]
        mine = gy.at[y, pl.ds(2 * xh, 2)]
        across = copies.start(mine, mine, member(1, 0, 0))
        arriving = {
            dy: [copies.start(mine, mine, member(0, 0, dy))] for dy in (1, 3, 2)
        }
        yield
        across.wait_recv()
        other = gy.at[y, pl.ds(2 - 2 * xh, 2)]
        for dy in (1, 3, 2):
            arriving[dy].append(copies.start(other, other, member(0, 0, dy)))
        piece_two(y)
        for dy in (1, 3, 2):
            yield
            for copy in arriving[dy]:
                copy.wait_recv()
            piece_two(lax.rem(y + NY - dy, NY))

    def stage_zeros():
        for q in range(2 * NZ):
            pz[q, :, WIDE:] = jnp.zeros((ONE, LANES - WIDE), BF16)
        for i in range(NY):
            local[i] = jnp.zeros((BAND, LANES), F32)
            rest_y[i, :, WIDE:] = jnp.zeros((FLOAT, LANES - WIDE), F32)
            for v in range(4):
                py[i, v, :, WIDE:] = jnp.zeros((TWO, LANES - WIDE), BF16)
                py[i, v, REAL:, :] = jnp.zeros((TWO - REAL, LANES), BF16)
        for i in range(2):
            gz[z, i, :, WIDE:] = jnp.zeros((ONE, LANES - WIDE), BF16)
        for v in range(2):
            gy[y, 2 * xh + v, :, WIDE:] = jnp.zeros((TWO, LANES - WIDE), BF16)

    def stage_pz(v):
        for r in range(4):
            q = 4 * v + r
            pz[q, :, 0:WIDE] = p_v[0:ONE, WIDE * q : WIDE * (q + 1)]

    def stage_py(v):
        for i in range(NY):
            for r in range(4):
                c = WIDE * (4 * v + r) + UNIT * i
                py[i, v, 0:REAL, UNIT * r : UNIT * (r + 1)] = p_v[ONE:ROWS, c : c + UNIT]

    def stage_mix():
        loads[2].wait()
        odd = lax.rem(lat, 2)
        first = pl.multiple_of(ROWS * lat - 4 * odd, 8)
        rows = m_v[pl.ds(first, ROWS + 4), :]
        rows = jnp.where(odd == 1, rows[4:], rows[:ROWS])
        mpad[...] = jnp.zeros((BAND, 4 * BAND), F32)
        for b in range(4):
            c = ROWS * b
            mpad[0:ROWS, ONE * b : ONE * (b + 1)] = rows[:, c : c + ONE]
            d = 4 * ONE + TWO * b
            mpad[0:ROWS, d : d + REAL] = rows[:, c + ONE : c + ROWS]
        for high, low, full in (
            (mh_one, ml_one, mpad[:, 0 : 4 * ONE]),
            (mh_two, ml_two, mpad[:, 4 * ONE :]),
        ):
            rounded = full.astype(BF16)
            high[...] = rounded
            low[...] = (full - rounded.astype(F32)).astype(BF16)

    def stage_lags():
        loads[1].wait()
        row = jnp.broadcast_to(weight[...].reshape(1, NWAVE), (8, NWAVE))
        work[...] = jnp.dot(
            row, e_v[...], precision=lax.Precision.HIGHEST, preferred_element_type=F32
        )

    def stage_kernel():
        for d in range(4):
            lags = jnp.concatenate(
                [
                    work[0:1, LEFT + WIDE * d : LEFT + WIDE * d + LANES],
                    work[0:1, WIDE * d : WIDE * d + LEFT],
                ],
                axis=1,
            )
            turned = pltpu.roll(
                jnp.broadcast_to(lags, (LANES, 2 * LANES)), 0, 1, stride=1, stride_axis=0
            )
            blocks[d] = turned[:, :LANES]

        def keep(high_ref, low_ref, place, block):
            high = block.astype(BF16)
            high_ref[place] = high
            low_ref[place] = (block - high.astype(F32)).astype(BF16)

        left, right = slice(0, LANES), slice(LANES, 2 * LANES)
        first, second = blocks[0] + blocks[2], blocks[1] + blocks[3]
        keep(sum_h, sum_l, (0,), (first + second) * 0.25)
        keep(sum_h, sum_l, (1,), (first - second) * 0.25)
        first, second = (blocks[0] - blocks[2]) * 0.5, (blocks[1] - blocks[3]) * 0.5
        keep(odd_h, odd_l, (left, left), first)
        keep(odd_h, odd_l, (right, right), first)
        keep(odd_h, odd_l, (left, right), second)
        keep(odd_h, odd_l, (right, left), -second)

    one, two = color_one(), color_two()
    next(one)
    next(two)
    stage_zeros()
    loads[0].wait()
    next(one)
    stage_pz(0)
    stage_pz(1)
    next(two)
    stage_pz(2)
    stage_pz(3)
    next(one)
    for k in range(4):
        stage_py(k)
    next(two)
    next(one)
    next(two)
    next(two)
    pass_piece(0)
    next(one)
    next(two, None)
    pass_piece(1)
    stage_mix()
    stage_lags()
    stage_kernel()
    pass_piece(2)
    next(one, None)
    pass_piece(3)
    mix_piece(0)
    mix_piece(1)
    pass_piece(4)
    mix_piece(2)
    mix_piece(3)
    for k in range(4, 8):
        if k + 1 < 8:
            pass_piece(k + 1)
        mix_piece(k)

    def product(value, high_ref, low_ref):
        high = value.astype(BF16)
        low = (value - high.astype(F32)).astype(BF16)
        return jnp.dot(high, high_ref, preferred_element_type=F32) + (
            jnp.dot(high, low_ref, preferred_element_type=F32)
            + jnp.dot(low, high_ref, preferred_element_type=F32)
        )

    even_0, even_1 = local[0] + local[2], local[1] + local[3]
    odd = jnp.concatenate([local[0] - local[2], local[1] - local[3]], axis=1)
    even_0, even_1 = (
        product(even_0 + even_1, sum_h[0], sum_l[0]),
        product(even_0 - even_1, sum_h[1], sum_l[1]),
    )
    even_0, even_1 = even_0 + even_1, even_0 - even_1
    odd_0 = product(odd, odd_h[:, 0:LANES], odd_l[:, 0:LANES])
    odd_1 = product(odd, odd_h[:, LANES:], odd_l[:, LANES:])
    rest[0] = even_0 + odd_0
    rest[1] = even_1 + odd_1
    rest[2] = even_0 - odd_0
    rest[3] = even_1 - odd_1

    def term_two(d, j):
        return py[d, j, 0:FLOAT].astype(F32) * rest_y[d]

    scale = 1.0 / math.sqrt(MEMBERS - 1)

    def sum_one(first, last, f1, s1, t1, p1):
        rows = slice(first, last)

        def term(d, j):
            return pz[j * NZ + d, rows].astype(F32) * rest[lax.rem(d, 4), rows]

        def store(j, value):
            for i in range(NY):
                t1[j, i, :, 0:UNIT] = value[:, UNIT * i : UNIT * (i + 1)]

        yield from scatter_ring(copies, NZ, z, term, f1, s1, 1, z_up, z_down, store)
        arriving = []
        for k, (dx, dy) in enumerate(plane):
            part = t1.at[lax.rem(xh + dx, 2), lax.rem(y + dy, NY)]
            arriving.append(copies.start(part, p1.at[k], member(dx, 0, dy)))
        yield
        total = t1[xh, y]
        for k, copy in enumerate(arriving):
            copy.wait_recv()
            total += p1[k]
        out[rows, :] = (total * scale)[:, 0:UNIT]

    def sum_two():
        for i in range(NY):
            for r in range(4):
                rest_y[i, :, UNIT * r : UNIT * (r + 1)] = rest[
                    r, ONE : ONE + FLOAT, UNIT * i : UNIT * (i + 1)
                ]
        arriving = []
        for k, (dx, dy) in enumerate(plane):
            to_x, to_y = lax.rem(xh + dx, 2), lax.rem(y + dy, NY)
            for i in range(2):
                f2[k, i] = term_two(to_y, 2 * to_x + i)
            arriving.append(copies.start(f2.at[k], s2.at[k], member(dx, 0, dy)))
        yield
        for i in range(2):
            total = term_two(y, 2 * xh + i)
            for k, copy in enumerate(arriving):
                if i == 0:
                    copy.wait_recv()
                total += s2[k, i]
            for r in range(4):
                t2[4 * i + r, :, 0:UNIT] = total[:, UNIT * r : UNIT * (r + 1)]
        arriving = []
        for k, dz in enumerate(turns):
            part = t2.at[lax.rem(z + dz, NZ)]
            arriving.append(copies.start(part, p2.at[k], member(0, dz, 0)))
        yield
        total = t2[z]
        for k, copy in enumerate(arriving):
            copy.wait_recv()
            total += p2[k]
        out[ONE:ROWS, :] = (total * scale)[0:REAL, 0:UNIT]

    one = sum_one(0, CUT, f1, s1, t1, p1)
    also = sum_one(CUT, ONE, f3, s3, t3, p3)
    two = sum_two()
    for chain in (one, also, two, one, also, one, also, one, also, two, one, also, two, one, also):
        next(chain, None)
    for copy in copies.made:
        copy.wait_send()


def local(gradient, perturbations, lat_mix, zonal_weight):
    vmem = pl.BlockSpec(memory_space=pltpu.VMEM)
    hbm = pl.BlockSpec(memory_space=pl.ANY)
    return pl.pallas_call(
        kernel,
        out_shape=jax.ShapeDtypeStruct((ROWS, UNIT), F32),
        in_specs=[hbm, vmem, hbm, vmem, hbm],
        out_specs=vmem,
        scratch_shapes=[
            pltpu.VMEM((ROWS, 4 * NLON), BF16),
            pltpu.VMEM((720, 720), F32),
            pltpu.VMEM((NWAVE, TABLE), F32),
            pltpu.VMEM((2, NY, ONE, 128), BF16),
            pltpu.VMEM((NZ, TWO, 128), BF16),
            pltpu.VMEM((NZ, 2, ONE, LANES), BF16),
            pltpu.VMEM((NY, 4, TWO, LANES), BF16),
            pltpu.VMEM((2 * NZ, ONE, LANES), BF16),
            pltpu.VMEM((NY, 4, TWO, LANES), BF16),
            pltpu.VMEM((8, TABLE), F32),
            pltpu.VMEM((BAND, LANES), F32),
            pltpu.VMEM((4, 4 * ONE, 2 * LANES), BF16),
            pltpu.VMEM((4, 4 * TWO, 2 * LANES), BF16),
            pltpu.VMEM((4, 4, ONE, 256), F32),
            pltpu.VMEM((4, 4, FLOAT, 256), F32),
            pltpu.VMEM((BAND, 4 * BAND), F32),
            pltpu.VMEM((BAND, 4 * ONE), BF16),
            pltpu.VMEM((BAND, 4 * ONE), BF16),
            pltpu.VMEM((BAND, 4 * TWO), BF16),
            pltpu.VMEM((BAND, 4 * TWO), BF16),
            pltpu.VMEM((4, LANES, LANES), F32),
            pltpu.VMEM((2, LANES, LANES), BF16),
            pltpu.VMEM((2, LANES, LANES), BF16),
            pltpu.VMEM((2 * LANES, 2 * LANES), BF16),
            pltpu.VMEM((2 * LANES, 2 * LANES), BF16),
            pltpu.VMEM((4, BAND, LANES), F32),
            pltpu.VMEM((4, BAND, LANES), F32),
            pltpu.VMEM((NY, FLOAT, LANES), F32),
            pltpu.VMEM((2, 2, CUT, LANES), F32),
            pltpu.VMEM((2, NZ // 2, 2, CUT, LANES), F32),
            pltpu.VMEM((2, NY, CUT, 128), F32),
            pltpu.VMEM((7, CUT, 128), F32),
            pltpu.VMEM((2, 2, ONE - CUT, LANES), F32),
            pltpu.VMEM((2, NZ // 2, 2, ONE - CUT, LANES), F32),
            pltpu.VMEM((2, NY, ONE - CUT, 128), F32),
            pltpu.VMEM((7, ONE - CUT, 128), F32),
            pltpu.VMEM((7, 2, FLOAT, LANES), F32),
            pltpu.VMEM((7, 2, FLOAT, LANES), F32),
            pltpu.VMEM((NZ, FLOAT, 128), F32),
            pltpu.VMEM((7, FLOAT, 128), F32),
            pltpu.SemaphoreType.DMA((3,)),
            pltpu.SemaphoreType.DMA((160,)),
            pltpu.SemaphoreType.DMA((160,)),
        ],
        compiler_params=pltpu.CompilerParams(
            collective_id=0, has_side_effects=True, vmem_limit_bytes=56 * 2**20
        ),
    )(
        perturbations.reshape(ROWS, 4 * NLON),
        gradient,
        lat_mix,
        zonal_weight,
        jnp.asarray(wave_table()),
    )


def solution(mesh):
    return jax.shard_map(
        local,
        mesh=mesh,
        in_specs=(P("lat", "mem"), P("mem", "lat", None), P(), P()),
        out_specs=P("lat", "mem"),
        check_vma=False,
    )
```

```python
import math

import jax
import jax.numpy as jnp
import numpy as np
from jax import lax
from jax.experimental import pallas as pl
from jax.experimental.pallas import tpu as pltpu
from jax.sharding import PartitionSpec as P

MESH = pl.DeviceIdType.MESH
F32 = jnp.float32
BF16 = jnp.bfloat16
NLON = 1440
NWAVE = 720
MEMBERS = 64
ROWS = 180
BAND = 192
ONE = 112
CUT = 64
TWO = BAND - ONE
REAL = ROWS - ONE
FLOAT = (REAL + 7) // 8 * 8
UNIT = 90
WIDE = 360
LANES = 384
FREE = WIDE - 256
NZ, NY = 8, 4
LEFT = 384
TABLE = 1920


def wave_table():
    waves = np.arange(NWAVE)
    offsets = np.arange(TABLE) - LEFT
    gains = np.where(waves == 0, 1.0, 2.0) / NLON
    angles = (waves[:, None] * offsets[None, :] % NLON) * (2.0 * math.pi / NLON)
    return (gains[:, None] * np.cos(angles)).astype(np.float32)


class Copies:
    def __init__(self, send, recv):
        self.send, self.recv, self.count, self.made = send, recv, 0, []

    def start(self, src, dst, device):
        k = self.count
        self.count += 1
        copy = pltpu.make_async_remote_copy(
            src_ref=src,
            dst_ref=dst,
            send_sem=self.send.at[k],
            recv_sem=self.recv.at[k],
            device_id=device,
            device_id_type=MESH,
        )
        copy.start()
        self.made.append(copy)
        return copy


def packed(value):
    lane = lax.broadcasted_iota(jnp.int32, (value.shape[0], 128), 1)
    most = jnp.max(jnp.abs(value), axis=1, keepdims=True)
    level = jnp.ceil(jnp.log(jnp.maximum(most, 1e-30) / 32000.0) * (8.0 / math.log(2.0)))
    whole = jnp.floor(value * jnp.exp(level * (-math.log(2.0) / 8.0)) + 0.5)
    a, b, c = whole[:, 0:128], whole[:, 128:256], whole[:, 256:384]
    c = jnp.where(lane < FREE, c, level)
    high = jnp.floor(b * (1.0 / 256.0) + 0.5)
    return jnp.concatenate([a * 256.0 + high, c * 256.0 + (b - high * 256.0)], axis=1)


def unpacked(words):
    lane = lax.broadcasted_iota(jnp.int32, (words.shape[0], 128), 1)
    first, second = words[:, 0:128], words[:, 128:256]
    a = jnp.floor(first * (1.0 / 256.0) + 0.5)
    c = jnp.floor(second * (1.0 / 256.0) + 0.5)
    b = (first - a * 256.0) * 256.0 + (second - c * 256.0)
    scale = jnp.exp(c[:, FREE : FREE + 1] * (math.log(2.0) / 8.0))
    c = jnp.where(lane < FREE, c, 0.0)
    return jnp.concatenate([a * scale, b * scale, c * scale], axis=1)


def gather_ring(copies, n, me, pick, parts, plus, minus):
    k = n // 2
    early, late = range(parts // 2), range(parts // 2, parts)
    up, down = {}, {}
    for i, j in zip((*early, *late), (*late, *early)):
        up[i] = copies.start(pick(me, i), pick(me, i), plus)
        down[j] = copies.start(pick(me, j), pick(me, j), minus)
    for t in range(1, k):
        yield t
        up_src, down_src = lax.rem(me - t + n, n), lax.rem(me + t, n)
        for i, j in zip((*early, *late), (*late, *early)):
            up[i].wait_recv()
            if t < k - 1 or i in early:
                up[i] = copies.start(pick(up_src, i), pick(up_src, i), plus)
            down[j].wait_recv()
            if t < k - 1 or j in late:
                down[j] = copies.start(pick(down_src, j), pick(down_src, j), minus)
    yield k
    for i, j in zip(early, late):
        up[i].wait_recv()
        down[j].wait_recv()


def scatter_ring(copies, n, me, own, first, slots, half, plus, minus, finish):
    k = n // 2
    low, high = range(half), range(half, 2 * half)
    up, down = {}, {}

    def begin(way, dest, j, t, device, made):
        first[way, j] = own(dest, j)
        made[j] = copies.start(first.at[way, j], slots.at[way, t, j], device)

    def forward(way, dest, j, t, device, made):
        made[j].wait_recv()
        slots[way, t - 1, j] += own(dest, j)
        made[j] = copies.start(slots.at[way, t - 1, j], slots.at[way, t, j], device)

    for a, b in zip(low, high):
        begin(0, lax.rem(me + k, n), a, 0, plus, up)
        begin(1, lax.rem(me + k, n), b, 0, minus, down)
    for a, b in zip(low, high):
        begin(0, lax.rem(me + k - 1, n), b, 1, plus, up)
        begin(1, lax.rem(me - k + 1 + n, n), a, 1, minus, down)
    for t in range(1, k):
        yield
        up_dest = lax.rem(me + k - t, n)
        down_dest = lax.rem(me - k + t + n, n)
        if t > 1:
            for a, b in zip(low, high):
                forward(0, up_dest, b, t, plus, up)
                forward(1, down_dest, a, t, minus, down)
        for a, b in zip(low, high):
            forward(0, up_dest, a, t, plus, up)
            forward(1, down_dest, b, t, minus, down)
    yield
    for j in (*high, *low):
        up[j].wait_recv()
        down[j].wait_recv()
        finish(j, slots[0, k - 1, j] + slots[1, k - 1, j] + own(me, j))


def kernel(
    pert, grad, mix, weight, table, out,
    p_v, m_v, e_v, yu, zu, gz, gy, pz, py, work, own_two, ag_one, ag_two, pk_one, pk_two,
    mpad, mh_one, ml_one, mh_two, ml_two, blocks, sum_h, sum_l, odd_h, odd_l, local, rest, rest_y,
    f1, s1, t1, p1, f3, s3, t3, p3, f2, s2, t2, p2,
    local_sem, send_sem, recv_sem,
):
    mem, lat = lax.axis_index("mem"), lax.axis_index("lat")
    xh, z, y = mem // 32, (mem // 4) % NZ, mem % NY

    def member(dx, dz, dy):
        there = (
            lax.rem(xh + dx, 2) * 32 + lax.rem(z + dz, NZ) * 4 + lax.rem(y + dy, NY)
        )
        return {"mem": there, "lat": lat}

    z_up, z_down = member(0, 1, 0), member(0, NZ - 1, 0)
    chip_lat = lax.rem(lat + 2, 4)
    chip = {"mem": mem, "lat": chip_lat}
    core = {"mem": mem, "lat": lat + 1 - 2 * lax.rem(lat, 2)}
    plane = [(1, 2), (0, 2), (1, 1), (1, 3), (0, 1), (0, 3), (1, 0)]
    turns = (4, 3, 5, 2, 6, 1, 7)
    copies = Copies(send_sem, recv_sem)

    loads = [
        pltpu.make_async_copy(pert, p_v, local_sem.at[0]),
        pltpu.make_async_copy(table, e_v, local_sem.at[1]),
        pltpu.make_async_copy(mix, m_v, local_sem.at[2]),
    ]
    for load in loads:
        load.start()

    barrier = pltpu.get_barrier_semaphore()
    peers = [member(dx, 0, dy) for dx, dy in plane]
    peers += [member(0, dz, 0) for dz in turns] + [chip, core]
    for peer in peers:
        pl.semaphore_signal(barrier, inc=1, device_id=peer, device_id_type=MESH)
    yu[xh, y] = jnp.zeros((ONE, 128), BF16)
    yu[xh, y, :, 0:UNIT] = grad[0:ONE]
    zu[z] = jnp.zeros((TWO, 128), BF16)
    zu[z, 0:REAL, 0:UNIT] = grad[ONE:ROWS]
    pl.semaphore_wait(barrier, len(peers))

    pieces = []

    def band_rows(b, rows):
        return pl.ds(pl.multiple_of(b * rows, 16), rows)

    def send_piece(first, index, value):
        ag, pack = (ag_one, pk_one) if first else (ag_two, pk_two)
        rows, sent = value.shape[0], pack.shape[2]
        pack[index, lat] = packed(value[0:sent])
        here = pack.at[index, lat]
        over = copies.start(here, here, chip)
        high = value.astype(BF16)
        ag[index, band_rows(lat, rows), 0:LANES] = high
        ag[index, band_rows(lat, rows), LANES:] = (value - high.astype(F32)).astype(BF16)
        here = ag.at[index, band_rows(lat, rows)]
        pieces.append(
            {
                "index": index,
                "one": first,
                "ag": ag,
                "pack": pack,
                "rows": rows,
                "chip": over,
                "core": copies.start(here, here, core),
            }
        )

    def unpack_piece(piece, b):
        value = unpacked(piece["pack"][piece["index"], b])
        rows, sent = piece["rows"], value.shape[0]
        if sent < rows:
            value = jnp.concatenate([value, jnp.zeros((rows - sent, LANES), F32)], axis=0)
        high = value.astype(BF16)
        low = (value - high.astype(F32)).astype(BF16)
        piece["ag"][piece["index"], band_rows(b, rows), 0:LANES] = high
        piece["ag"][piece["index"], band_rows(b, rows), LANES:] = low

    def pass_piece(k):
        piece = pieces[k]
        piece["chip"].wait_recv()
        there = piece["pack"].at[piece["index"], chip_lat]
        piece["passed"] = copies.start(there, there, core)
        unpack_piece(piece, chip_lat)

    def mixed(high, low, ag, index):
        both = jnp.dot(high[...], ag[index], preferred_element_type=F32)
        return both[:, :LANES] + (
            both[:, LANES:]
            + jnp.dot(low[...], ag[index, :, 0:LANES], preferred_element_type=F32)
        )

    def mix_piece(k):
        piece = pieces[k]
        piece["core"].wait_recv()
        piece["passed"].wait_recv()
        unpack_piece(piece, chip_lat + 1 - 2 * lax.rem(lat, 2))
        index = piece["index"]
        if piece["one"]:
            local[index] += mixed(mh_one, ml_one, ag_one, index)
        else:
            work_y[...] = mixed(mh_two, ml_two, ag_two, index)
            for i in range(NY):

                @pl.when(index == i)
                def _():
                    for r in range(4):
                        local[r, :, UNIT * i : UNIT * (i + 1)] += work_y[
                            :, UNIT * r : UNIT * (r + 1)
                        ]

    work_y = own_two

    def piece_one(r):
        total = jnp.zeros((ONE, LANES), F32)
        for v in range(4):
            total += pz[4 * v + r].astype(F32) * gz[r + 4 * (v % 2), v // 2].astype(F32)
        send_piece(True, r, total)
        local[r, 0:ONE] += total

    def piece_two(i):
        total = jnp.zeros((TWO, LANES), F32)
        for v in range(4):
            total += py[i, v].astype(F32) * gy[i, v].astype(F32)
        send_piece(False, i, total)
        own_two[0:TWO] = total
        for i_ in range(NY):

            @pl.when(i == i_)
            def _():
                for r in range(4):
                    local[r, ONE:BAND, UNIT * i_ : UNIT * (i_ + 1)] += own_two[
                        0:TWO, UNIT * r : UNIT * (r + 1)
                    ]

    def color_one():
        mine = yu.at[xh, y]
        arriving = [copies.start(mine, mine, member(dx, 0, dy)) for dx, dy in plane]
        yield
        for copy in arriving:
            copy.wait_recv()
        for i in range(2):
            for j in range(NY):
                gz[z, i, :, UNIT * j : UNIT * (j + 1)] = yu[i, j, :, 0:UNIT]
        cuts = (pl.ds(0, CUT), pl.ds(CUT, ONE - CUT))

        def pick(d, part):
            return gz.at[d, part // 2, cuts[part % 2]]

        for t in gather_ring(copies, NZ, z, pick, 4, z_up, z_down):
            if t == 3:
                piece_one(lax.rem(z + 2, 4))
            if t == 4:
                piece_one(lax.rem(z + 1, 4))
                piece_one(lax.rem(z + 3, 4))
            yield
        piece_one(lax.rem(z, 4))

    def color_two():
        mine = zu.at[z]
        arriving = [copies.start(mine, mine, member(0, dz, 0)) for dz in turns]
        yield
        for copy in arriving:
            copy.wait_recv()
        for i in range(2):
            for r in range(4):
                gy[y, 2 * xh + i, :, UNIT * r : UNIT * (r + 1)] = zu[4 * i + r, :, 0:UNIT]
        mine = gy.at[y, pl.ds(2 * xh, 2)]
        across = copies.start(mine, mine, member(1, 0, 0))
        arriving = {
            dy: [copies.start(mine, mine, member(0, 0, dy))] for dy in (1, 3, 2)
        }
        yield
        across.wait_recv()
        other = gy.at[y, pl.ds(2 - 2 * xh, 2)]
        for dy in (1, 3, 2):
            arriving[dy].append(copies.start(other, other, member(0, 0, dy)))
        piece_two(y)
        for dy in (1, 3, 2):
            yield
            for copy in arriving[dy]:
                copy.wait_recv()
            piece_two(lax.rem(y + NY - dy, NY))

    def stage_zeros():
        for q in range(2 * NZ):
            pz[q, :, WIDE:] = jnp.zeros((ONE, LANES - WIDE), BF16)
        for i in range(NY):
            local[i] = jnp.zeros((BAND, LANES), F32)
            rest_y[i, :, WIDE:] = jnp.zeros((FLOAT, LANES - WIDE), F32)
            for v in range(4):
                py[i, v, :, WIDE:] = jnp.zeros((TWO, LANES - WIDE), BF16)
                py[i, v, REAL:, :] = jnp.zeros((TWO - REAL, LANES), BF16)
        for i in range(2):
            gz[z, i, :, WIDE:] = jnp.zeros((ONE, LANES - WIDE), BF16)
        for v in range(2):
            gy[y, 2 * xh + v, :, WIDE:] = jnp.zeros((TWO, LANES - WIDE), BF16)

    def stage_pz(v):
        for r in range(4):
            q = 4 * v + r
            pz[q, :, 0:WIDE] = p_v[0:ONE, WIDE * q : WIDE * (q + 1)]

    def stage_py(v):
        for i in range(NY):
            for r in range(4):
                c = WIDE * (4 * v + r) + UNIT * i
                py[i, v, 0:REAL, UNIT * r : UNIT * (r + 1)] = p_v[ONE:ROWS, c : c + UNIT]

    def stage_mix():
        loads[2].wait()
        odd = lax.rem(lat, 2)
        first = pl.multiple_of(ROWS * lat - 4 * odd, 8)
        rows = m_v[pl.ds(first, ROWS + 4), :]
        rows = jnp.where(odd == 1, rows[4:], rows[:ROWS])
        mpad[...] = jnp.zeros((BAND, 4 * BAND), F32)
        for b in range(4):
            c = ROWS * b
            mpad[0:ROWS, ONE * b : ONE * (b + 1)] = rows[:, c : c + ONE]
            d = 4 * ONE + TWO * b
            mpad[0:ROWS, d : d + REAL] = rows[:, c + ONE : c + ROWS]
        for high, low, full in (
            (mh_one, ml_one, mpad[:, 0 : 4 * ONE]),
            (mh_two, ml_two, mpad[:, 4 * ONE :]),
        ):
            rounded = full.astype(BF16)
            high[...] = rounded
            low[...] = (full - rounded.astype(F32)).astype(BF16)

    def stage_lags():
        loads[1].wait()
        row = jnp.broadcast_to(weight[...].reshape(1, NWAVE), (8, NWAVE))
        work[...] = jnp.dot(
            row, e_v[...], precision=lax.Precision.HIGHEST, preferred_element_type=F32
        )

    def stage_kernel():
        for d in range(4):
            lags = jnp.concatenate(
                [
                    work[0:1, LEFT + WIDE * d : LEFT + WIDE * d + LANES],
                    work[0:1, WIDE * d : WIDE * d + LEFT],
                ],
                axis=1,
            )
            turned = pltpu.roll(
                jnp.broadcast_to(lags, (LANES, 2 * LANES)), 0, 1, stride=1, stride_axis=0
            )
            blocks[d] = turned[:, :LANES]

        def keep(high_ref, low_ref, place, block):
            high = block.astype(BF16)
            high_ref[place] = high
            low_ref[place] = (block - high.astype(F32)).astype(BF16)

        left, right = slice(0, LANES), slice(LANES, 2 * LANES)
        first, second = blocks[0] + blocks[2], blocks[1] + blocks[3]
        keep(sum_h, sum_l, (0,), (first + second) * 0.25)
        keep(sum_h, sum_l, (1,), (first - second) * 0.25)
        first, second = (blocks[0] - blocks[2]) * 0.5, (blocks[1] - blocks[3]) * 0.5
        keep(odd_h, odd_l, (left, left), first)
        keep(odd_h, odd_l, (right, right), first)
        keep(odd_h, odd_l, (left, right), second)
        keep(odd_h, odd_l, (right, left), -second)

    one, two = color_one(), color_two()
    next(one)
    next(two)
    stage_zeros()
    loads[0].wait()
    next(one)
    stage_pz(0)
    stage_pz(1)
    next(two)
    stage_pz(2)
    stage_pz(3)
    next(one)
    for k in range(4):
        stage_py(k)
    next(two)
    next(one)
    next(two)
    next(two)
    pass_piece(0)
    next(one)
    next(two, None)
    pass_piece(1)
    stage_mix()
    stage_lags()
    stage_kernel()
    pass_piece(2)
    next(one, None)
    pass_piece(3)
    mix_piece(0)
    mix_piece(1)
    pass_piece(4)
    pass_piece(5)
    mix_piece(2)
    mix_piece(3)
    pass_piece(6)
    mix_piece(4)
    mix_piece(5)
    pass_piece(7)
    mix_piece(6)
    mix_piece(7)

    def product(value, high_ref, low_ref):
        high = value.astype(BF16)
        low = (value - high.astype(F32)).astype(BF16)
        return jnp.dot(high, high_ref, preferred_element_type=F32) + (
            jnp.dot(high, low_ref, preferred_element_type=F32)
            + jnp.dot(low, high_ref, preferred_element_type=F32)
        )

    even_0, even_1 = local[0] + local[2], local[1] + local[3]
    odd = jnp.concatenate([local[0] - local[2], local[1] - local[3]], axis=1)
    even_0, even_1 = (
        product(even_0 + even_1, sum_h[0], sum_l[0]),
        product(even_0 - even_1, sum_h[1], sum_l[1]),
    )
    even_0, even_1 = even_0 + even_1, even_0 - even_1
    odd_0 = product(odd, odd_h[:, 0:LANES], odd_l[:, 0:LANES])
    odd_1 = product(odd, odd_h[:, LANES:], odd_l[:, LANES:])
    rest[0] = even_0 + odd_0
    rest[1] = even_1 + odd_1
    rest[2] = even_0 - odd_0
    rest[3] = even_1 - odd_1

    def term_two(d, j):
        return py[d, j, 0:FLOAT].astype(F32) * rest_y[d]

    scale = 1.0 / math.sqrt(MEMBERS - 1)

    def sum_one(first, last, f1, s1, t1, p1):
        rows = slice(first, last)

        def term(d, j):
            return pz[j * NZ + d, rows].astype(F32) * rest[lax.rem(d, 4), rows]

        def store(j, value):
            for i in range(NY):
                t1[j, i, :, 0:UNIT] = value[:, UNIT * i : UNIT * (i + 1)]

        yield from scatter_ring(copies, NZ, z, term, f1, s1, 1, z_up, z_down, store)
        arriving = []
        for k, (dx, dy) in enumerate(plane):
            part = t1.at[lax.rem(xh + dx, 2), lax.rem(y + dy, NY)]
            arriving.append(copies.start(part, p1.at[k], member(dx, 0, dy)))
        yield
        total = t1[xh, y]
        for k, copy in enumerate(arriving):
            copy.wait_recv()
            total += p1[k]
        out[rows, :] = (total * scale)[:, 0:UNIT]

    def sum_two():
        for i in range(NY):
            for r in range(4):
                rest_y[i, :, UNIT * r : UNIT * (r + 1)] = rest[
                    r, ONE : ONE + FLOAT, UNIT * i : UNIT * (i + 1)
                ]
        arriving = []
        for k, (dx, dy) in enumerate(plane):
            to_x, to_y = lax.rem(xh + dx, 2), lax.rem(y + dy, NY)
            for i in range(2):
                f2[k, i] = term_two(to_y, 2 * to_x + i)
            arriving.append(copies.start(f2.at[k], s2.at[k], member(dx, 0, dy)))
        yield
        for i in range(2):
            total = term_two(y, 2 * xh + i)
            for k, copy in enumerate(arriving):
                if i == 0:
                    copy.wait_recv()
                total += s2[k, i]
            for r in range(4):
                t2[4 * i + r, :, 0:UNIT] = total[:, UNIT * r : UNIT * (r + 1)]
        arriving = []
        for k, dz in enumerate(turns):
            part = t2.at[lax.rem(z + dz, NZ)]
            arriving.append(copies.start(part, p2.at[k], member(0, dz, 0)))
        yield
        total = t2[z]
        for k, copy in enumerate(arriving):
            copy.wait_recv()
            total += p2[k]
        out[ONE:ROWS, :] = (total * scale)[0:REAL, 0:UNIT]

    one = sum_one(0, CUT, f1, s1, t1, p1)
    also = sum_one(CUT, ONE, f3, s3, t3, p3)
    two = sum_two()
    for chain in (one, also, two, one, also, one, also, one, also, two, one, also, two, one, also):
        next(chain, None)
    for copy in copies.made:
        copy.wait_send()


def local(gradient, perturbations, lat_mix, zonal_weight):
    vmem = pl.BlockSpec(memory_space=pltpu.VMEM)
    hbm = pl.BlockSpec(memory_space=pl.ANY)
    return pl.pallas_call(
        kernel,
        out_shape=jax.ShapeDtypeStruct((ROWS, UNIT), F32),
        in_specs=[hbm, vmem, hbm, vmem, hbm],
        out_specs=vmem,
        scratch_shapes=[
            pltpu.VMEM((ROWS, 4 * NLON), BF16),
            pltpu.VMEM((720, 720), F32),
            pltpu.VMEM((NWAVE, TABLE), F32),
            pltpu.VMEM((2, NY, ONE, 128), BF16),
            pltpu.VMEM((NZ, TWO, 128), BF16),
            pltpu.VMEM((NZ, 2, ONE, LANES), BF16),
            pltpu.VMEM((NY, 4, TWO, LANES), BF16),
            pltpu.VMEM((2 * NZ, ONE, LANES), BF16),
            pltpu.VMEM((NY, 4, TWO, LANES), BF16),
            pltpu.VMEM((8, TABLE), F32),
            pltpu.VMEM((BAND, LANES), F32),
            pltpu.VMEM((4, 4 * ONE, 2 * LANES), BF16),
            pltpu.VMEM((4, 4 * TWO, 2 * LANES), BF16),
            pltpu.VMEM((4, 4, ONE, 256), F32),
            pltpu.VMEM((4, 4, FLOAT, 256), F32),
            pltpu.VMEM((BAND, 4 * BAND), F32),
            pltpu.VMEM((BAND, 4 * ONE), BF16),
            pltpu.VMEM((BAND, 4 * ONE), BF16),
            pltpu.VMEM((BAND, 4 * TWO), BF16),
            pltpu.VMEM((BAND, 4 * TWO), BF16),
            pltpu.VMEM((4, LANES, LANES), F32),
            pltpu.VMEM((2, LANES, LANES), BF16),
            pltpu.VMEM((2, LANES, LANES), BF16),
            pltpu.VMEM((2 * LANES, 2 * LANES), BF16),
            pltpu.VMEM((2 * LANES, 2 * LANES), BF16),
            pltpu.VMEM((4, BAND, LANES), F32),
            pltpu.VMEM((4, BAND, LANES), F32),
            pltpu.VMEM((NY, FLOAT, LANES), F32),
            pltpu.VMEM((2, 2, CUT, LANES), F32),
            pltpu.VMEM((2, NZ // 2, 2, CUT, LANES), F32),
            pltpu.VMEM((2, NY, CUT, 128), F32),
            pltpu.VMEM((7, CUT, 128), F32),
            pltpu.VMEM((2, 2, ONE - CUT, LANES), F32),
            pltpu.VMEM((2, NZ // 2, 2, ONE - CUT, LANES), F32),
            pltpu.VMEM((2, NY, ONE - CUT, 128), F32),
            pltpu.VMEM((7, ONE - CUT, 128), F32),
            pltpu.VMEM((7, 2, FLOAT, LANES), F32),
            pltpu.VMEM((7, 2, FLOAT, LANES), F32),
            pltpu.VMEM((NZ, FLOAT, 128), F32),
            pltpu.VMEM((7, FLOAT, 128), F32),
            pltpu.SemaphoreType.DMA((3,)),
            pltpu.SemaphoreType.DMA((160,)),
            pltpu.SemaphoreType.DMA((160,)),
        ],
        compiler_params=pltpu.CompilerParams(
            collective_id=0, has_side_effects=True, vmem_limit_bytes=56 * 2**20
        ),
    )(
        perturbations.reshape(ROWS, 4 * NLON),
        gradient,
        lat_mix,
        zonal_weight,
        jnp.asarray(wave_table()),
    )


def solution(mesh):
    return jax.shard_map(
        local,
        mesh=mesh,
        in_specs=(P("lat", "mem"), P("mem", "lat", None), P(), P()),
        out_specs=P("lat", "mem"),
        check_vma=False,
    )
```

```python
import math

import jax
import jax.numpy as jnp
import numpy as np
from jax import lax
from jax.experimental import pallas as pl
from jax.experimental.pallas import tpu as pltpu
from jax.sharding import PartitionSpec as P

MESH = pl.DeviceIdType.MESH
F32 = jnp.float32
BF16 = jnp.bfloat16
NLON = 1440
NWAVE = 720
MEMBERS = 64
ROWS = 180
BAND = 192
ONE = 112
CUT = 64
TWO = BAND - ONE
REAL = ROWS - ONE
FLOAT = (REAL + 7) // 8 * 8
UNIT = 90
WIDE = 360
LANES = 384
FREE = WIDE - 256
NZ, NY = 8, 4
LEFT = 384
TABLE = 1920


def wave_table():
    waves = np.arange(NWAVE)
    offsets = np.arange(TABLE) - LEFT
    gains = np.where(waves == 0, 1.0, 2.0) / NLON
    angles = (waves[:, None] * offsets[None, :] % NLON) * (2.0 * math.pi / NLON)
    return (gains[:, None] * np.cos(angles)).astype(np.float32)


class Copies:
    def __init__(self, send, recv):
        self.send, self.recv, self.count, self.made = send, recv, 0, []

    def start(self, src, dst, device):
        k = self.count
        self.count += 1
        copy = pltpu.make_async_remote_copy(
            src_ref=src,
            dst_ref=dst,
            send_sem=self.send.at[k],
            recv_sem=self.recv.at[k],
            device_id=device,
            device_id_type=MESH,
        )
        copy.start()
        self.made.append(copy)
        return copy


def packed(value):
    lane = lax.broadcasted_iota(jnp.int32, (value.shape[0], 128), 1)
    most = jnp.max(jnp.abs(value), axis=1, keepdims=True)
    level = jnp.ceil(jnp.log(jnp.maximum(most, 1e-30) / 32000.0) * (8.0 / math.log(2.0)))
    whole = jnp.floor(value * jnp.exp(level * (-math.log(2.0) / 8.0)) + 0.5)
    a, b, c = whole[:, 0:128], whole[:, 128:256], whole[:, 256:384]
    c = jnp.where(lane < FREE, c, level)
    high = jnp.floor(b * (1.0 / 256.0) + 0.5)
    return jnp.concatenate([a * 256.0 + high, c * 256.0 + (b - high * 256.0)], axis=1)


def unpacked(words):
    lane = lax.broadcasted_iota(jnp.int32, (words.shape[0], 128), 1)
    first, second = words[:, 0:128], words[:, 128:256]
    a = jnp.floor(first * (1.0 / 256.0) + 0.5)
    c = jnp.floor(second * (1.0 / 256.0) + 0.5)
    b = (first - a * 256.0) * 256.0 + (second - c * 256.0)
    scale = jnp.exp(c[:, FREE : FREE + 1] * (math.log(2.0) / 8.0))
    c = jnp.where(lane < FREE, c, 0.0)
    return jnp.concatenate([a * scale, b * scale, c * scale], axis=1)


def gather_ring(copies, n, me, pick, parts, plus, minus):
    k = n // 2
    early, late = range(parts // 2), range(parts // 2, parts)
    up, down = {}, {}
    for i, j in zip((*early, *late), (*late, *early)):
        up[i] = copies.start(pick(me, i), pick(me, i), plus)
        down[j] = copies.start(pick(me, j), pick(me, j), minus)
    for t in range(1, k):
        yield t
        up_src, down_src = lax.rem(me - t + n, n), lax.rem(me + t, n)
        for i, j in zip((*early, *late), (*late, *early)):
            up[i].wait_recv()
            if t < k - 1 or i in early:
                up[i] = copies.start(pick(up_src, i), pick(up_src, i), plus)
            down[j].wait_recv()
            if t < k - 1 or j in late:
                down[j] = copies.start(pick(down_src, j), pick(down_src, j), minus)
    yield k
    for i, j in zip(early, late):
        up[i].wait_recv()
        down[j].wait_recv()


def scatter_ring(copies, n, me, own, first, slots, half, plus, minus, finish):
    k = n // 2
    low, high = range(half), range(half, 2 * half)
    up, down = {}, {}

    def begin(way, dest, j, t, device, made):
        first[way, j] = own(dest, j)
        made[j] = copies.start(first.at[way, j], slots.at[way, t, j], device)

    def forward(way, dest, j, t, device, made):
        made[j].wait_recv()
        slots[way, t - 1, j] += own(dest, j)
        made[j] = copies.start(slots.at[way, t - 1, j], slots.at[way, t, j], device)

    for a, b in zip(low, high):
        begin(0, lax.rem(me + k, n), a, 0, plus, up)
        begin(1, lax.rem(me + k, n), b, 0, minus, down)
    for a, b in zip(low, high):
        begin(0, lax.rem(me + k - 1, n), b, 1, plus, up)
        begin(1, lax.rem(me - k + 1 + n, n), a, 1, minus, down)
    for t in range(1, k):
        yield
        up_dest = lax.rem(me + k - t, n)
        down_dest = lax.rem(me - k + t + n, n)
        if t > 1:
            for a, b in zip(low, high):
                forward(0, up_dest, b, t, plus, up)
                forward(1, down_dest, a, t, minus, down)
        for a, b in zip(low, high):
            forward(0, up_dest, a, t, plus, up)
            forward(1, down_dest, b, t, minus, down)
    yield
    for j in (*high, *low):
        up[j].wait_recv()
        down[j].wait_recv()
        finish(j, slots[0, k - 1, j] + slots[1, k - 1, j] + own(me, j))


def kernel(
    pert, grad, mix, weight, table, out,
    p_v, m_v, e_v, yu, zu, gz, gy, pz, py, work, own_two, ag_one, ag_two, pk_one, pk_two,
    mpad, mh_one, ml_one, mh_two, ml_two, blocks, sum_h, sum_l, odd_h, odd_l, local, rest, rest_y,
    f1, s1, t1, p1, f3, s3, t3, p3, f2, s2, t2, p2,
    local_sem, send_sem, recv_sem,
):
    mem, lat = lax.axis_index("mem"), lax.axis_index("lat")
    xh, z, y = mem // 32, (mem // 4) % NZ, mem % NY

    def member(dx, dz, dy):
        there = (
            lax.rem(xh + dx, 2) * 32 + lax.rem(z + dz, NZ) * 4 + lax.rem(y + dy, NY)
        )
        return {"mem": there, "lat": lat}

    z_up, z_down = member(0, 1, 0), member(0, NZ - 1, 0)
    chip_lat = lax.rem(lat + 2, 4)
    chip = {"mem": mem, "lat": chip_lat}
    core = {"mem": mem, "lat": lat + 1 - 2 * lax.rem(lat, 2)}
    plane = [(1, 2), (0, 2), (1, 1), (1, 3), (0, 1), (0, 3), (1, 0)]
    turns = (4, 3, 5, 2, 6, 1, 7)
    copies = Copies(send_sem, recv_sem)

    loads = [
        pltpu.make_async_copy(pert, p_v, local_sem.at[0]),
        pltpu.make_async_copy(table, e_v, local_sem.at[1]),
        pltpu.make_async_copy(mix, m_v, local_sem.at[2]),
    ]
    for load in loads:
        load.start()

    barrier = pltpu.get_barrier_semaphore()
    peers = [member(dx, 0, dy) for dx, dy in plane]
    peers += [member(0, dz, 0) for dz in turns] + [chip, core]
    for peer in peers:
        pl.semaphore_signal(barrier, inc=1, device_id=peer, device_id_type=MESH)
    yu[xh, y] = jnp.zeros((ONE, 128), BF16)
    yu[xh, y, :, 0:UNIT] = grad[0:ONE]
    zu[z] = jnp.zeros((TWO, 128), BF16)
    zu[z, 0:REAL, 0:UNIT] = grad[ONE:ROWS]
    pl.semaphore_wait(barrier, len(peers))

    pieces = []

    def band_rows(b, rows):
        return pl.ds(pl.multiple_of(b * rows, 16), rows)

    def send_piece(first, index, value):
        ag, pack = (ag_one, pk_one) if first else (ag_two, pk_two)
        rows, sent = value.shape[0], pack.shape[2]
        pack[index, lat] = packed(value[0:sent])
        here = pack.at[index, lat]
        over = copies.start(here, here, chip)
        high = value.astype(BF16)
        ag[index, band_rows(lat, rows), 0:LANES] = high
        ag[index, band_rows(lat, rows), LANES:] = (value - high.astype(F32)).astype(BF16)
        here = ag.at[index, band_rows(lat, rows)]
        pieces.append(
            {
                "index": index,
                "one": first,
                "ag": ag,
                "pack": pack,
                "rows": rows,
                "chip": over,
                "core": copies.start(here, here, core),
            }
        )

    def unpack_piece(piece, b):
        value = unpacked(piece["pack"][piece["index"], b])
        rows, sent = piece["rows"], value.shape[0]
        if sent < rows:
            value = jnp.concatenate([value, jnp.zeros((rows - sent, LANES), F32)], axis=0)
        high = value.astype(BF16)
        low = (value - high.astype(F32)).astype(BF16)
        piece["ag"][piece["index"], band_rows(b, rows), 0:LANES] = high
        piece["ag"][piece["index"], band_rows(b, rows), LANES:] = low

    def pass_piece(k):
        piece = pieces[k]
        piece["chip"].wait_recv()
        there = piece["pack"].at[piece["index"], chip_lat]
        piece["passed"] = copies.start(there, there, core)
        unpack_piece(piece, chip_lat)

    def mixed(high, low, ag, index):
        both = jnp.dot(high[...], ag[index], preferred_element_type=F32)
        return both[:, :LANES] + (
            both[:, LANES:]
            + jnp.dot(low[...], ag[index, :, 0:LANES], preferred_element_type=F32)
        )

    def mix_piece(k):
        piece = pieces[k]
        piece["core"].wait_recv()
        piece["passed"].wait_recv()
        unpack_piece(piece, chip_lat + 1 - 2 * lax.rem(lat, 2))
        index = piece["index"]
        if piece["one"]:
            local[index] += mixed(mh_one, ml_one, ag_one, index)
        else:
            work_y[...] = mixed(mh_two, ml_two, ag_two, index)
            for i in range(NY):

                @pl.when(index == i)
                def _():
                    for r in range(4):
                        local[r, :, UNIT * i : UNIT * (i + 1)] += work_y[
                            :, UNIT * r : UNIT * (r + 1)
                        ]

    work_y = own_two

    def piece_one(r):
        total = jnp.zeros((ONE, LANES), F32)
        for v in range(4):
            total += pz[4 * v + r].astype(F32) * gz[r + 4 * (v % 2), v // 2].astype(F32)
        send_piece(True, r, total)
        local[r, 0:ONE] += total

    def piece_two(i):
        total = jnp.zeros((TWO, LANES), F32)
        for v in range(4):
            total += py[i, v].astype(F32) * gy[i, v].astype(F32)
        send_piece(False, i, total)
        own_two[0:TWO] = total
        for i_ in range(NY):

            @pl.when(i == i_)
            def _():
                for r in range(4):
                    local[r, ONE:BAND, UNIT * i_ : UNIT * (i_ + 1)] += own_two[
                        0:TWO, UNIT * r : UNIT * (r + 1)
                    ]

    def color_one():
        mine = yu.at[xh, y]
        arriving = [copies.start(mine, mine, member(dx, 0, dy)) for dx, dy in plane]
        yield
        for copy in arriving:
            copy.wait_recv()
        for i in range(2):
            for j in range(NY):
                gz[z, i, :, UNIT * j : UNIT * (j + 1)] = yu[i, j, :, 0:UNIT]
        cuts = (pl.ds(0, CUT), pl.ds(CUT, ONE - CUT))

        def pick(d, part):
            return gz.at[d, part // 2, cuts[part % 2]]

        for t in gather_ring(copies, NZ, z, pick, 4, z_up, z_down):
            if t == 3:
                piece_one(lax.rem(z + 2, 4))
            if t == 4:
                piece_one(lax.rem(z + 1, 4))
                piece_one(lax.rem(z + 3, 4))
            yield
        piece_one(lax.rem(z, 4))

    def color_two():
        mine = zu.at[z]
        arriving = [copies.start(mine, mine, member(0, dz, 0)) for dz in turns]
        yield
        for copy in arriving:
            copy.wait_recv()
        for i in range(2):
            for r in range(4):
                gy[y, 2 * xh + i, :, UNIT * r : UNIT * (r + 1)] = zu[4 * i + r, :, 0:UNIT]
        mine = gy.at[y, pl.ds(2 * xh, 2)]
        across = copies.start(mine, mine, member(1, 0, 0))
        arriving = {
            dy: [copies.start(mine, mine, member(0, 0, dy))] for dy in (1, 3, 2)
        }
        yield
        across.wait_recv()
        other = gy.at[y, pl.ds(2 - 2 * xh, 2)]
        for dy in (1, 3, 2):
            arriving[dy].append(copies.start(other, other, member(0, 0, dy)))
        piece_two(y)
        for dy in (1, 3, 2):
            yield
            for copy in arriving[dy]:
                copy.wait_recv()
            piece_two(lax.rem(y + NY - dy, NY))

    def stage_zeros():
        for q in range(2 * NZ):
            pz[q, :, WIDE:] = jnp.zeros((ONE, LANES - WIDE), BF16)
        for i in range(NY):
            local[i] = jnp.zeros((BAND, LANES), F32)
            rest_y[i, :, WIDE:] = jnp.zeros((FLOAT, LANES - WIDE), F32)
            for v in range(4):
                py[i, v, :, WIDE:] = jnp.zeros((TWO, LANES - WIDE), BF16)
                py[i, v, REAL:, :] = jnp.zeros((TWO - REAL, LANES), BF16)
        for i in range(2):
            gz[z, i, :, WIDE:] = jnp.zeros((ONE, LANES - WIDE), BF16)
        for v in range(2):
            gy[y, 2 * xh + v, :, WIDE:] = jnp.zeros((TWO, LANES - WIDE), BF16)

    def stage_pz(v):
        for r in range(4):
            q = 4 * v + r
            pz[q, :, 0:WIDE] = p_v[0:ONE, WIDE * q : WIDE * (q + 1)]

    def stage_py(v):
        for i in range(NY):
            for r in range(4):
                c = WIDE * (4 * v + r) + UNIT * i
                py[i, v, 0:REAL, UNIT * r : UNIT * (r + 1)] = p_v[ONE:ROWS, c : c + UNIT]

    def stage_mix():
        loads[2].wait()
        odd = lax.rem(lat, 2)
        first = pl.multiple_of(ROWS * lat - 4 * odd, 8)
        rows = m_v[pl.ds(first, ROWS + 4), :]
        rows = jnp.where(odd == 1, rows[4:], rows[:ROWS])
        mpad[...] = jnp.zeros((BAND, 4 * BAND), F32)
        for b in range(4):
            c = ROWS * b
            mpad[0:ROWS, ONE * b : ONE * (b + 1)] = rows[:, c : c + ONE]
            d = 4 * ONE + TWO * b
            mpad[0:ROWS, d : d + REAL] = rows[:, c + ONE : c + ROWS]
        for high, low, full in (
            (mh_one, ml_one, mpad[:, 0 : 4 * ONE]),
            (mh_two, ml_two, mpad[:, 4 * ONE :]),
        ):
            rounded = full.astype(BF16)
            high[...] = rounded
            low[...] = (full - rounded.astype(F32)).astype(BF16)

    def stage_lags():
        loads[1].wait()
        row = jnp.broadcast_to(weight[...].reshape(1, NWAVE), (8, NWAVE))
        work[...] = jnp.dot(
            row, e_v[...], precision=lax.Precision.HIGHEST, preferred_element_type=F32
        )

    def stage_kernel():
        for d in range(4):
            lags = jnp.concatenate(
                [
                    work[0:1, LEFT + WIDE * d : LEFT + WIDE * d + LANES],
                    work[0:1, WIDE * d : WIDE * d + LEFT],
                ],
                axis=1,
            )
            turned = pltpu.roll(
                jnp.broadcast_to(lags, (LANES, 2 * LANES)), 0, 1, stride=1, stride_axis=0
            )
            blocks[d] = turned[:, :LANES]

        def keep(high_ref, low_ref, place, block):
            high = block.astype(BF16)
            high_ref[place] = high
            low_ref[place] = (block - high.astype(F32)).astype(BF16)

        left, right = slice(0, LANES), slice(LANES, 2 * LANES)
        first, second = blocks[0] + blocks[2], blocks[1] + blocks[3]
        keep(sum_h, sum_l, (0,), (first + second) * 0.25)
        keep(sum_h, sum_l, (1,), (first - second) * 0.25)
        first, second = (blocks[0] - blocks[2]) * 0.5, (blocks[1] - blocks[3]) * 0.5
        keep(odd_h, odd_l, (left, left), first)
        keep(odd_h, odd_l, (right, right), first)
        keep(odd_h, odd_l, (left, right), second)
        keep(odd_h, odd_l, (right, left), -second)

    one, two = color_one(), color_two()
    next(one)
    next(two)
    stage_zeros()
    loads[0].wait()
    next(one)
    stage_pz(0)
    stage_pz(1)
    next(two)
    stage_pz(2)
    stage_pz(3)
    next(one)
    for k in range(4):
        stage_py(k)
    next(two)
    next(one)
    next(two)
    next(two)
    pass_piece(0)
    next(one)
    next(two, None)
    stage_lags()
    stage_kernel()
    pass_piece(1)
    stage_mix()
    pass_piece(2)
    next(one, None)
    pass_piece(3)
    mix_piece(0)
    mix_piece(1)
    pass_piece(4)
    mix_piece(2)
    mix_piece(3)
    for k in range(4, 8):
        if k + 1 < 8:
            pass_piece(k + 1)
        mix_piece(k)

    def product(value, high_ref, low_ref):
        high = value.astype(BF16)
        low = (value - high.astype(F32)).astype(BF16)
        return jnp.dot(high, high_ref, preferred_element_type=F32) + (
            jnp.dot(high, low_ref, preferred_element_type=F32)
            + jnp.dot(low, high_ref, preferred_element_type=F32)
        )

    even_0, even_1 = local[0] + local[2], local[1] + local[3]
    odd = jnp.concatenate([local[0] - local[2], local[1] - local[3]], axis=1)
    even_0, even_1 = (
        product(even_0 + even_1, sum_h[0], sum_l[0]),
        product(even_0 - even_1, sum_h[1], sum_l[1]),
    )
    even_0, even_1 = even_0 + even_1, even_0 - even_1
    odd_0 = product(odd, odd_h[:, 0:LANES], odd_l[:, 0:LANES])
    odd_1 = product(odd, odd_h[:, LANES:], odd_l[:, LANES:])
    rest[0] = even_0 + odd_0
    rest[1] = even_1 + odd_1
    rest[2] = even_0 - odd_0
    rest[3] = even_1 - odd_1

    def term_two(d, j):
        return py[d, j, 0:FLOAT].astype(F32) * rest_y[d]

    scale = 1.0 / math.sqrt(MEMBERS - 1)

    def sum_one(first, last, f1, s1, t1, p1):
        rows = slice(first, last)

        def term(d, j):
            return pz[j * NZ + d, rows].astype(F32) * rest[lax.rem(d, 4), rows]

        def store(j, value):
            for i in range(NY):
                t1[j, i, :, 0:UNIT] = value[:, UNIT * i : UNIT * (i + 1)]

        yield from scatter_ring(copies, NZ, z, term, f1, s1, 1, z_up, z_down, store)
        arriving = []
        for k, (dx, dy) in enumerate(plane):
            part = t1.at[lax.rem(xh + dx, 2), lax.rem(y + dy, NY)]
            arriving.append(copies.start(part, p1.at[k], member(dx, 0, dy)))
        yield
        total = t1[xh, y]
        for k, copy in enumerate(arriving):
            copy.wait_recv()
            total += p1[k]
        out[rows, :] = (total * scale)[:, 0:UNIT]

    def sum_two():
        for i in range(NY):
            for r in range(4):
                rest_y[i, :, UNIT * r : UNIT * (r + 1)] = rest[
                    r, ONE : ONE + FLOAT, UNIT * i : UNIT * (i + 1)
                ]
        arriving = []
        for k, (dx, dy) in enumerate(plane):
            to_x, to_y = lax.rem(xh + dx, 2), lax.rem(y + dy, NY)
            for i in range(2):
                f2[k, i] = term_two(to_y, 2 * to_x + i)
            arriving.append(copies.start(f2.at[k], s2.at[k], member(dx, 0, dy)))
        yield
        for i in range(2):
            total = term_two(y, 2 * xh + i)
            for k, copy in enumerate(arriving):
                if i == 0:
                    copy.wait_recv()
                total += s2[k, i]
            for r in range(4):
                t2[4 * i + r, :, 0:UNIT] = total[:, UNIT * r : UNIT * (r + 1)]
        arriving = []
        for k, dz in enumerate(turns):
            part = t2.at[lax.rem(z + dz, NZ)]
            arriving.append(copies.start(part, p2.at[k], member(0, dz, 0)))
        yield
        total = t2[z]
        for k, copy in enumerate(arriving):
            copy.wait_recv()
            total += p2[k]
        out[ONE:ROWS, :] = (total * scale)[0:REAL, 0:UNIT]

    one = sum_one(0, CUT, f1, s1, t1, p1)
    also = sum_one(CUT, ONE, f3, s3, t3, p3)
    two = sum_two()
    for chain in (one, also, two, one, also, one, also, one, also, two, one, also, two, one, also):
        next(chain, None)
    for copy in copies.made:
        copy.wait_send()


def local(gradient, perturbations, lat_mix, zonal_weight):
    vmem = pl.BlockSpec(memory_space=pltpu.VMEM)
    hbm = pl.BlockSpec(memory_space=pl.ANY)
    return pl.pallas_call(
        kernel,
        out_shape=jax.ShapeDtypeStruct((ROWS, UNIT), F32),
        in_specs=[hbm, vmem, hbm, vmem, hbm],
        out_specs=vmem,
        scratch_shapes=[
            pltpu.VMEM((ROWS, 4 * NLON), BF16),
            pltpu.VMEM((720, 720), F32),
            pltpu.VMEM((NWAVE, TABLE), F32),
            pltpu.VMEM((2, NY, ONE, 128), BF16),
            pltpu.VMEM((NZ, TWO, 128), BF16),
            pltpu.VMEM((NZ, 2, ONE, LANES), BF16),
            pltpu.VMEM((NY, 4, TWO, LANES), BF16),
            pltpu.VMEM((2 * NZ, ONE, LANES), BF16),
            pltpu.VMEM((NY, 4, TWO, LANES), BF16),
            pltpu.VMEM((8, TABLE), F32),
            pltpu.VMEM((BAND, LANES), F32),
            pltpu.VMEM((4, 4 * ONE, 2 * LANES), BF16),
            pltpu.VMEM((4, 4 * TWO, 2 * LANES), BF16),
            pltpu.VMEM((4, 4, ONE, 256), F32),
            pltpu.VMEM((4, 4, FLOAT, 256), F32),
            pltpu.VMEM((BAND, 4 * BAND), F32),
            pltpu.VMEM((BAND, 4 * ONE), BF16),
            pltpu.VMEM((BAND, 4 * ONE), BF16),
            pltpu.VMEM((BAND, 4 * TWO), BF16),
            pltpu.VMEM((BAND, 4 * TWO), BF16),
            pltpu.VMEM((4, LANES, LANES), F32),
            pltpu.VMEM((2, LANES, LANES), BF16),
            pltpu.VMEM((2, LANES, LANES), BF16),
            pltpu.VMEM((2 * LANES, 2 * LANES), BF16),
            pltpu.VMEM((2 * LANES, 2 * LANES), BF16),
            pltpu.VMEM((4, BAND, LANES), F32),
            pltpu.VMEM((4, BAND, LANES), F32),
            pltpu.VMEM((NY, FLOAT, LANES), F32),
            pltpu.VMEM((2, 2, CUT, LANES), F32),
            pltpu.VMEM((2, NZ // 2, 2, CUT, LANES), F32),
            pltpu.VMEM((2, NY, CUT, 128), F32),
            pltpu.VMEM((7, CUT, 128), F32),
            pltpu.VMEM((2, 2, ONE - CUT, LANES), F32),
            pltpu.VMEM((2, NZ // 2, 2, ONE - CUT, LANES), F32),
            pltpu.VMEM((2, NY, ONE - CUT, 128), F32),
            pltpu.VMEM((7, ONE - CUT, 128), F32),
            pltpu.VMEM((7, 2, FLOAT, LANES), F32),
            pltpu.VMEM((7, 2, FLOAT, LANES), F32),
            pltpu.VMEM((NZ, FLOAT, 128), F32),
            pltpu.VMEM((7, FLOAT, 128), F32),
            pltpu.SemaphoreType.DMA((3,)),
            pltpu.SemaphoreType.DMA((160,)),
            pltpu.SemaphoreType.DMA((160,)),
        ],
        compiler_params=pltpu.CompilerParams(
            collective_id=0, has_side_effects=True, vmem_limit_bytes=56 * 2**20
        ),
    )(
        perturbations.reshape(ROWS, 4 * NLON),
        gradient,
        lat_mix,
        zonal_weight,
        jnp.asarray(wave_table()),
    )


def solution(mesh):
    return jax.shard_map(
        local,
        mesh=mesh,
        in_specs=(P("lat", "mem"), P("mem", "lat", None), P(), P()),
        out_specs=P("lat", "mem"),
        check_vma=False,
    )
```
